256 devices in a mesh: rep: 32 (over z_lo, y, core), fsdp: 8 (over x, z_hi).
Axes of the slice: x: 4, y: 4, z: 8 (z_hi: 2, z_lo: 4; z = z_hi * 4 + z_lo), core: 2. Of those that a mesh axis runs over, the one named last changes fastest.
Arguments:
- inputs: bfloat16 [65536, 8192], P(('rep', 'fsdp')), may hold values from -24 to 24
- cotangent: bfloat16 [65536, 1024], P(('rep', 'fsdp')), may hold values from -6 to 6
- codes: bfloat16 [8192, 1024], P('fsdp'), may hold values from -4 to 4
- scales: bfloat16 [128, 1024], P('fsdp'), may hold values from 0.0049743652 to 0.019897461
- adapter_down: bfloat16 [64, 8192], P(None, 'fsdp'), may hold values from -0.0625 to 0.0625
- adapter_up: bfloat16 [64, 1024], replicated, may hold values from -0.75 to 0.75
Outputs:
- values_out: bfloat16 [65536, 1024], P(('rep', 'fsdp'))
- input_grad: bfloat16 [65536, 8192], P(('rep', 'fsdp'))
- down_grad: float32 [64, 8192], P(None, 'fsdp')
- up_grad: float32 [64, 1024], replicated
The draws below stay inside these ranges and needn't reach their ends.
All inputs are finite; a program needn't handle non-finite values.
Results may differ from the reference program's by a relative error of at most 0.0095.
Values may be sent and summed in bfloat16 or wider, within the bound.
A program may use at most 128 MiB of HBM per device.

```python
import math
import jax
import jax.numpy as jnp

D = 8192
KV = 1024
RANK = 64
BLOCK = 64
TOKENS = 65536


def spiked(array, rng, source, target, blocks, factor):
    owner, partner = [(jnp.arange(array.shape[dim]) // (array.shape[dim] // blocks)).reshape([-1 if axis == dim else 1 for axis in range(array.ndim)]) for dim in (source, target)]
    chosen = jax.random.permutation(rng, blocks)[partner]
    strong = (owner == chosen) | (owner == (partner + blocks // 2) % blocks)
    return jnp.where(strong, factor * array, array)


def block_scale(stream_key, shape, shards, least, top_value):
    def one(axis_at, shards_of):
        heights = jax.random.uniform(jax.random.fold_in(jax.random.fold_in(stream_key, 6), axis_at), (shards_of,), jnp.float32, least / len(shards), top_value / len(shards))
        return jnp.repeat(jnp.exp(heights), shape[axis_at] // shards_of).reshape((-1,) + (1,) * (len(shape) - axis_at - 1))

    loudness = one(*shards[0])
    for cut in shards[1:]:
        loudness = loudness * one(*cut)
    return loudness


def scatter_about(stream_key, extent, scale, limit, shards=(), kind=jnp.bfloat16):
    values = scale * jax.random.normal(stream_key, extent, jnp.float32)
    if shards:
        values = values * block_scale(stream_key, extent, shards, -0.22, 0.18)
    return jnp.clip(values, -limit, limit).astype(kind)


def noise_with(stream_key, shape, spread, bound, pieces, heavy, kind=jnp.bfloat16):
    result = spread * jax.random.normal(stream_key, shape, jnp.float32)
    if pieces:
        result = result * block_scale(stream_key, shape, pieces, -0.22, 0.18)
    return jnp.clip(spiked(result, jax.random.fold_in(stream_key, 3), *heavy), -bound, bound).astype(kind)


def setup_inputs(seed: int = 0) -> dict:
    key_of = jax.random.split(jax.random.key(seed), 7)
    inputs = noise_with(key_of[0], (TOKENS, D), 1.0, 24.0, ((0, 256),), (0, 1, 256, 6.0))
    cotangent = scatter_about(key_of[1], (TOKENS, KV), 1.0, 6.0, ((0, 256),))
    codes = scatter_about(key_of[2], (D, KV), 1.0, 4.0, ((0, 8),))
    scales = jnp.clip(jnp.exp(math.log(0.019897461) - 1.3862944 * jax.random.uniform(key_of[3], (D // BLOCK, KV), jnp.float32) ** block_scale(key_of[3], (D // BLOCK, KV), ((0, 8),), -0.2, 0.2)), 0.0049743652, 0.019897461).astype(jnp.bfloat16)
    adapter_down = scatter_about(key_of[4], (RANK, D), D ** -0.5, 0.0625, ((1, 8),))
    adapter_up = scatter_about(key_of[5], (RANK, KV), RANK ** -0.5, 0.75)
    return {"inputs": inputs, "cotangent": cotangent, "codes": codes, "scales": scales, "adapter_down": adapter_down, "adapter_up": adapter_up}


def dequantize(codes, scales):
    blocks = codes.astype(jnp.float32).reshape(D // BLOCK, BLOCK, KV) * scales.astype(jnp.float32)[:, None, :]
    return blocks.reshape(D, KV).astype(jnp.bfloat16)

def reference(inputs, cotangent, codes, scales, adapter_down, adapter_up):
    weight = dequantize(codes, scales)
    low = jnp.dot(inputs, adapter_down.T, preferred_element_type=jnp.float32).astype(jnp.bfloat16)
    values_out = (jnp.dot(inputs, weight, preferred_element_type=jnp.float32) + 2.0 * jnp.dot(low, adapter_up, preferred_element_type=jnp.float32)).astype(jnp.bfloat16)
    back = (2.0 * jnp.dot(cotangent, adapter_up.T, preferred_element_type=jnp.float32)).astype(jnp.bfloat16)
    input_grad = (jnp.dot(cotangent, weight.T, preferred_element_type=jnp.float32) + jnp.dot(back, adapter_down, preferred_element_type=jnp.float32)).astype(jnp.bfloat16)
    raw_up = 2.0 * jnp.dot(low.T, cotangent, preferred_element_type=jnp.float32)
    raw_down = jnp.dot(back.T, inputs, preferred_element_type=jnp.float32)
    total = jnp.sqrt(jnp.sum(raw_down * raw_down) + jnp.sum(raw_up * raw_up))
    factor = jnp.minimum(jnp.float32(1.0), math.sqrt(RANK * (D + KV)) / total)
    return (values_out, input_grad, factor * raw_down, factor * raw_up)
```

```python
import functools
import math

import jax
import jax.numpy as jnp
from jax import lax
from jax.experimental import pallas as pl
from jax.experimental.pallas import tpu as pltpu
from jax.sharding import PartitionSpec as P

MESH = pl.DeviceIdType.MESH
F32, BF16 = jnp.float32, jnp.bfloat16
UNIT = 64
EXT = 1152
N_SEND, N_RECV = 128, 128


def nn(a, b):
    return jnp.dot(a, b, preferred_element_type=F32)


def nt(a, b):
    return lax.dot_general(a, b, (((1,), (1,)), ((), ())), preferred_element_type=F32)


def kernel(
    limit,
    x_hbm, g_hbm, codes_hbm, scales_hbm, down_hbm, up_hbm,
    val_hbm, ig_hbm, dg_hbm, ug_hbm,
    inp, cot, cod, scl, scf, upv, wt, dn, raw, g1, a2, b2, s2, a3, b3, s3, a4, b4, t5, e6, f7,
    ig, vacc, vout, back, back_t, low, low_t, dgo, ugo,
    load_sem, out_sem, send_sem, recv_sem,
):
    rep, fs_me = lax.axis_index("rep"), lax.axis_index("fsdp")
    c = lax.rem(rep, 2)
    y = lax.rem(lax.div(rep, 2), 4)
    zl = lax.div(rep, 8)
    x = lax.div(fs_me, 2)
    zh = lax.rem(fs_me, 2)
    r = lax.rem(lax.rem(zl, 2) + lax.div(zl, 2), 2)
    zp = zl + 1 - 2 * lax.rem(zl, 2)

    def dev(dx=0, dy=0, zl_=zl, zh_=zh, c_=c):
        return {
            "rep": (zl_ * 4 + lax.rem(y + dy + 4, 4)) * 2 + c_,
            "fsdp": lax.rem(x + dx + 4, 4) * 2 + zh_,
        }

    sibling = dev(c_=1 - c)
    pair = dev(zl_=zp)
    mirror = dev(zl_=3 - zl, zh_=1 - zh)

    def same(dx):
        return lax.rem(x + dx + 4, 4) * 2 + zh

    def other(dx):
        return lax.rem(x + dx + 4, 4) * 2 + (1 - zh)

    names, sends = {}, []

    def sem(*key):
        return recv_sem.at[names.setdefault(key, len(names))]

    def send(ref, device, *key, dst=None):
        copy = pltpu.make_async_remote_copy(
            src_ref=ref,
            dst_ref=ref if dst is None else dst,
            send_sem=send_sem.at[len(sends)],
            recv_sem=sem(*key),
            device_id=device,
            device_id_type=MESH,
        )
        copy.start()
        sends.append(copy)

    def arrive(ref, *key):
        pltpu.make_async_copy(ref, ref, sem(*key)).wait()

    half = c * 512
    loads = {}

    def load(name, src, dst):
        loads[name] = pltpu.make_async_copy(src, dst, load_sem.at[len(loads)])
        loads[name].start()

    rows_mine, rows_sib = pl.ds(pl.multiple_of(half, 512), 512), pl.ds(pl.multiple_of(512 - half, 512), 512)
    load("scales", scales_hbm, scl)
    load("codes", codes_hbm.at[rows_mine], cod.at[rows_mine])
    load("down", down_hbm, dn.at[fs_me])
    load("up", up_hbm, upv)
    load("cot", g_hbm, cot)
    for f in range(8):
        load(("x", f), x_hbm.at[:, pl.ds(f * 1024, 1024)], inp.at[f])
    load("codes2", codes_hbm.at[rows_sib], cod.at[rows_sib])

    peers = [sibling, pair]
    peers += [dev(dx=d) for d in (1, 2, 3)]
    peers += [dev(dx=d, zl_=3 - zl, zh_=1 - zh) for d in range(4)]
    peers += [dev(dy=d) for d in (1, 2, 3)]
    peers += [dev(dy=d, zl_=3 - zl) for d in range(4)]
    barrier = pltpu.get_barrier_semaphore()
    for peer in peers:
        pl.semaphore_signal(barrier, inc=1, device_id=peer, device_id_type=MESH)

    def dequantize(block):
        rows = pl.ds(pl.multiple_of(block * UNIT, UNIT), UNIT)
        wt[fs_me, rows, :] = (cod[rows, :].astype(F32) * scf[pl.ds(block, 1), :]).astype(BF16)

    def unit(f, u, n=1):
        return wt.at[f, pl.ds(pl.multiple_of(half + u * UNIT, UNIT), n * UNIT)]

    u_me, u_pair = 2 * y + r, 2 * y + 1 - r

    def chunk(d):
        return 2 * lax.rem(y + d + 4, 4)

    pieces = [(u_me, 1), (u_pair, 1), (chunk(1), 2), (chunk(2), 2), (chunk(3), 2)]
    loads["scales"].wait()
    scf[...] = scl[...].astype(F32)
    loads["codes"].wait()
    dequantize(c * 8 + u_me)
    loads["down"].wait()
    pl.semaphore_wait(barrier, len(peers))

    cols_mine = pl.ds(pl.multiple_of(half, 512), 512)
    cols_sib = pl.ds(pl.multiple_of(512 - half, 512), 512)

    def dpart(f, cols=cols_mine):
        return dn.at[f, :, cols]

    for d in (1, 3, 2):
        send(dpart(fs_me), dev(dx=d), "d1", d)

    def x_send(m):
        for way in (1, -1):
            send(unit(fs_me, *pieces[m]), dev(dx=way), "x", way, m)

    def x_arrive(m):
        for way in (1, -1):
            arrive(unit(same(-way), *pieces[m]), "x", way, m)

    x_send(0)
    send(unit(fs_me, u_me), mirror, "z", 0)
    dequantize(c * 8 + u_pair)
    x_send(1)

    @pl.loop(1, 4)
    def _(d):
        for k in range(2):
            dequantize(c * 8 + 2 * lax.rem(y + d, 4) + k)

    loads["cot"].wait()
    loads["up"].wait()
    back[...] = (2.0 * nt(cot[...], upv[...])).astype(BF16)
    back_t[...] = (2.0 * nt(upv[...], cot[...])).astype(BF16)
    for f in range(8):
        loads[("x", f)].wait()

    def down_term(f):
        raw[f, :, 0:1024] = nn(back_t[...], inp[f])

    def z_send(dx):
        send(unit(same(dx), u_me), mirror, "z", dx)

    def z_arrive(dx):
        arrive(unit(other(dx), u_me), "z", dx)
        send(unit(other(dx), u_me), pair, "p", dx)
        for way in (1, -1):
            send(unit(other(dx), u_me), dev(dy=way), "y0", way, dx)

    def p_arrive(dx):
        arrive(unit(other(dx), u_pair), "p", dx)
        for way in (1, -1):
            send(unit(other(dx), u_pair), dev(dy=way), "y1", way, dx)

    def y0_arrive(dx):
        for way in (1, -1):
            arrive(unit(other(dx), chunk(-way) + r), "y0", way, dx)
        send(unit(other(dx), chunk(-1) + r), dev(dy=1), "yf0", dx)

    def y1_arrive(dx):
        for way in (1, -1):
            arrive(unit(other(dx), chunk(-way) + 1 - r), "y1", way, dx)
        send(unit(other(dx), chunk(1) + 1 - r), dev(dy=-1), "yf1", dx)

    def yf_arrive(dx):
        arrive(unit(other(dx), chunk(2) + r), "yf0", dx)
        arrive(unit(other(dx), chunk(2) + 1 - r), "yf1", dx)

    def forward(way, m, first=0, n=None):
        u, size = pieces[m]
        send(unit(same(-way), u + first, n or size), dev(dx=way), "xf", m, first)

    def far_arrive(m, first=0, n=None):
        u, size = pieces[m]
        arrive(unit(same(2), u + first, n or size), "xf", m, first)

    def share(f, *key):
        send(wt.at[f, rows_mine], sibling, "c", *key)

    def shared(f, *key):
        arrive(wt.at[f, rows_sib], "c", *key)

    outs = []

    def out(src, dst):
        copy = pltpu.make_async_copy(src, dst, out_sem.at[len(outs)])
        copy.start()
        outs.append(copy)

    def multiply(f, first=False):
        @pl.loop(0, 4)
        def _(n):
            cols = pl.ds(pl.multiple_of(n * 256, 256), 256)
            term = nn(inp[f], wt[f, :, cols])
            vacc[:, cols] = term if first else vacc[:, cols] + term

        @pl.loop(0, 4)
        def _(n):
            rows = pl.ds(pl.multiple_of(n * 256, 256), 256)
            ig[f, :, rows] = (nt(cot[...], wt[f, rows, :]) + nn(back[...], dn[f, :, rows])).astype(BF16)

        out(ig.at[f], ig_hbm.at[:, pl.ds(pl.multiple_of(f * 1024, 1024), 1024)])

    for d in (1, 3, 2):
        arrive(dpart(same(-d)), "d1", d)
    send(dpart(y * 2 + zh), mirror, "d2")
    for d in (1, 2, 3):
        send(dpart(same(-d)), sibling, "d4", d)

    x_arrive(0)
    forward(1, 0)
    z_send(-1)
    z_send(1)
    x_send(2)
    pl.loop(0, 8)(down_term)
    arrive(dpart(y * 2 + 1 - zh), "d2")
    for d in (1, 3, 2):
        send(dpart(y * 2 + 1 - zh), dev(dy=d), "d3", d)
    send(dpart(y * 2 + 1 - zh), sibling, "d4", 0)
    z_arrive(0)
    x_arrive(1)
    forward(-1, 1)
    x_send(3)
    far_arrive(0)
    z_send(2)
    p_arrive(0)
    for d in (1, 3, 2):
        arrive(dpart(lax.rem(y - d + 4, 4) * 2 + 1 - zh), "d3", d)
        send(dpart(lax.rem(y - d + 4, 4) * 2 + 1 - zh), sibling, "d4", 3 + d)
    z_arrive(-1)
    z_arrive(1)

    for d in (1, 2, 3):
        arrive(dpart(same(-d), cols_sib), "d4", d)
    arrive(dpart(y * 2 + 1 - zh, cols_sib), "d4", 0)
    for d in (1, 2, 3):
        arrive(dpart(lax.rem(y - d + 4, 4) * 2 + 1 - zh, cols_sib), "d4", 3 + d)
    low[...] = jnp.zeros_like(low)
    low_t[...] = jnp.zeros_like(low_t)

    @pl.loop(0, 8)
    def _(f):
        low[...] += nt(inp[f], dn[f])
        low_t[...] += nt(dn[f], inp[f])

    up_term = 2.0 * nn(low_t[...].astype(BF16), cot[...])
    for f in range(8):
        raw[f, :, 1024:EXT] = up_term[:, f * 128 : f * 128 + 128]
    send(raw.at[:, pl.ds(pl.multiple_of(32 - c * 32, 32), 32), :], sibling, "g1", dst=g1)

    x_arrive(2)
    forward(1, 2)
    x_send(4)
    y0_arrive(0)

    arrive(g1, "g1")
    keep, give = pl.ds(pl.multiple_of(r * 16, 16), 16), pl.ds(pl.multiple_of(16 - r * 16, 16), 16)
    keep_c = pl.ds(pl.multiple_of(c * 32 + r * 16, 16), 16)
    give_c = pl.ds(pl.multiple_of(c * 32 + 16 - r * 16, 16), 16)

    @pl.loop(0, 8)
    def _(f):
        a2[f] = (raw[f, give_c, :] + g1[f, give, :]).astype(BF16)
        s2[f] = raw[f, keep_c, :] + g1[f, keep, :]

    send(a2, pair, "g2", dst=b2)
    p_arrive(-1)
    p_arrive(1)
    loads["codes2"].wait()

    @pl.loop(0, 8)
    def _(k):
        dequantize((1 - c) * 8 + k)

    multiply(fs_me, first=True)
    z_arrive(2)
    arrive(b2, "g2")
    for k in range(4):
        a3[k] = (s2[k * 2 + 1 - zh] + b2[k * 2 + 1 - zh].astype(F32)).astype(BF16)
        s3[k] = s2[k * 2 + zh] + b2[k * 2 + zh].astype(F32)
    send(a3, mirror, "g3", dst=b3)
    x_arrive(3)
    forward(-1, 3)
    y1_arrive(0)
    y0_arrive(-1)
    y0_arrive(1)
    arrive(b3, "g3")
    for d in (1, 2, 3):
        k = lax.rem(x + d, 4)
        a4[d - 1] = (s3[k] + b3[k].astype(F32)).astype(BF16)
        send(a4.at[d - 1], dev(dx=d), "g4", d, dst=b4.at[d - 1])
    p_arrive(2)
    x_arrive(4)
    forward(1, 4, 0, 1)
    forward(-1, 4, 1, 1)
    share(same(-1), "s", -1)
    share(same(1), "s", 1)
    total = s3[x] + b3[x].astype(F32)
    for d in (1, 2, 3):
        arrive(b4.at[d - 1], "g4", d)
        total += b4[d - 1].astype(F32)
    mine = y * 2 + lax.div(zl, 2)
    t5[mine] = total.astype(BF16)
    group = [(d, flip) for d in range(4) for flip in range(2) if d or flip]
    for d, flip in group:
        send(t5.at[mine], dev(dy=d, zl_=3 - zl if flip else zl), "g5", d, flip)
    y1_arrive(-1)
    y1_arrive(1)
    yf_arrive(0)
    share(other(0), "o", 0)

    for d, flip in group:
        at = lax.rem(y - d + 4, 4) * 2 + (1 - lax.div(zl, 2) if flip else lax.div(zl, 2))
        arrive(t5.at[at], "g5", d, flip)
    total = t5[0].astype(F32)
    for k in range(1, 8):
        total += t5[k].astype(F32)
    square = total * total
    square = square[0:8] + square[8:16]
    tile = square[:, 0:128]
    for k in range(1, 9):
        tile += square[:, k * 128 : k * 128 + 128]
    q = c * 2 + r
    e6[fs_me, 0:16, :] = total[:, 1024:EXT]
    e6[fs_me, 16:24, :] = tile
    f7[q, 0:16, :] = total[:, 0:1024]
    group = [(d, flip) for d in range(4) for flip in range(2) if d or flip]
    for d, flip in group:
        device = dev(dx=d, zl_=3 - zl, zh_=1 - zh) if flip else dev(dx=d)
        send(e6.at[fs_me], device, "g6", d, flip)
    y0_arrive(2)
    shared(same(-1), "s", -1)
    shared(same(1), "s", 1)
    multiply(same(-1))
    multiply(same(1))
    for d, flip in group:
        at = other(-d) if flip else same(-d)
        arrive(e6.at[at], "g6", d, flip)
    tile = e6[0, 16:24, :]
    for f in range(8):
        f7[q, 16:32, f * 128 : f * 128 + 128] = e6[f, 0:16, :]
        if f:
            tile += e6[f, 16:24, :]
    f7[q, 32:40, 0:128] = tile
    f7[q, 32:40, 128:1024] = jnp.zeros((8, 896), F32)
    send(f7.at[q], pair, "g7")
    y1_arrive(2)
    for m, first, n in ((1, 0, 1), (2, 0, 2), (3, 0, 2), (4, 0, 1), (4, 1, 1)):
        far_arrive(m, first, n)
    share(same(2), "s", 2)
    yf_arrive(-1)
    yf_arrive(1)
    share(other(-1), "o", -1)
    share(other(1), "o", 1)
    arrive(f7.at[c * 2 + 1 - r], "g7")
    send(f7.at[pl.ds(c * 2, 2)], sibling, "g8")
    shared(other(0), "o", 0)
    multiply(other(0))
    shared(same(2), "s", 2)
    multiply(same(2))
    yf_arrive(2)
    share(other(2), "o", 2)
    for dx in (-1, 1):
        shared(other(dx), "o", dx)
        multiply(other(dx))
    arrive(f7.at[pl.ds(2 - c * 2, 2)], "g8")
    tile = f7[0, 32:40, 0:128]
    for k in range(1, 4):
        tile += f7[k, 32:40, 0:128]
    squares = jnp.sum(jnp.sum(tile, axis=1, keepdims=True), axis=0, keepdims=True)
    factor = jnp.minimum(1.0, limit / jnp.sqrt(squares))
    for k in range(4):
        dgo[k * 16 : k * 16 + 16, :] = factor * f7[k, 0:16, :]
        ugo[k * 16 : k * 16 + 16, :] = factor * f7[k, 16:32, :]
    out(dgo, dg_hbm)
    out(ugo, ug_hbm)
    shared(other(2), "o", 2)
    multiply(other(2))
    vout[...] = (vacc[...] + 2.0 * nn(low[...].astype(BF16), upv[...])).astype(BF16)
    out(vout, val_hbm)
    for copy in sends:
        copy.wait_send()
    for copy in outs:
        copy.wait()
    assert len(names) <= N_RECV and len(sends) <= N_SEND


def local(inputs, cotangent, codes, scales, adapter_down, adapter_up):
    rank, values_width = adapter_up.shape
    limit = math.sqrt(rank * (inputs.shape[1] + values_width))
    scratch = [
        pltpu.VMEM((8, 256, 1024), BF16),
        pltpu.VMEM((256, 1024), BF16),
        pltpu.VMEM((1024, 1024), BF16),
        pltpu.VMEM((16, 1024), BF16),
        pltpu.VMEM((16, 1024), F32),
        pltpu.VMEM((64, 1024), BF16),
        pltpu.VMEM((8, 1024, 1024), BF16),
        pltpu.VMEM((8, 64, 1024), BF16),
        pltpu.VMEM((8, 64, EXT), F32),
        pltpu.VMEM((8, 32, EXT), F32),
        pltpu.VMEM((8, 16, EXT), BF16),
        pltpu.VMEM((8, 16, EXT), BF16),
        pltpu.VMEM((8, 16, EXT), F32),
        pltpu.VMEM((4, 16, EXT), BF16),
        pltpu.VMEM((4, 16, EXT), BF16),
        pltpu.VMEM((4, 16, EXT), F32),
        pltpu.VMEM((3, 16, EXT), BF16),
        pltpu.VMEM((3, 16, EXT), BF16),
        pltpu.VMEM((8, 16, EXT), BF16),
        pltpu.VMEM((8, 24, 128), F32),
        pltpu.VMEM((4, 40, 1024), F32),
        pltpu.VMEM((8, 256, 1024), BF16),
        pltpu.VMEM((256, 1024), F32),
        pltpu.VMEM((256, 1024), BF16),
        pltpu.VMEM((256, 64), BF16),
        pltpu.VMEM((64, 256), BF16),
        pltpu.VMEM((256, 64), F32),
        pltpu.VMEM((64, 256), F32),
        pltpu.VMEM((64, 1024), F32),
        pltpu.VMEM((64, 1024), F32),
        pltpu.SemaphoreType.DMA((16,)),
        pltpu.SemaphoreType.DMA((16,)),
        pltpu.SemaphoreType.DMA((N_SEND,)),
        pltpu.SemaphoreType.DMA((N_RECV,)),
    ]
    hbm = pl.BlockSpec(memory_space=pl.ANY)
    return pl.pallas_call(
        functools.partial(kernel, limit),
        out_shape=(
            jax.ShapeDtypeStruct((256, 1024), BF16),
            jax.ShapeDtypeStruct((256, 8192), BF16),
            jax.ShapeDtypeStruct((64, 1024), F32),
            jax.ShapeDtypeStruct((64, 1024), F32),
        ),
        in_specs=[hbm] * 6,
        out_specs=(hbm,) * 4,
        scratch_shapes=scratch,
        cost_estimate=pl.CostEstimate(flops=9_600_000_000, bytes_accessed=12_000_000, transcendentals=0),
        compiler_params=pltpu.CompilerParams(
            collective_id=0, has_side_effects=True, vmem_limit_bytes=56 << 20
        ),
    )(inputs, cotangent, codes, scales, adapter_down, adapter_up)


def solution(mesh):
    return jax.shard_map(
        local,
        mesh=mesh,
        in_specs=(
            P(("rep", "fsdp"), None),
            P(("rep", "fsdp"), None),
            P("fsdp", None),
            P("fsdp", None),
            P(None, "fsdp"),
            P(),
        ),
        out_specs=(P(("rep", "fsdp"), None), P(("rep", "fsdp"), None), P(None, "fsdp"), P()),
        check_vma=False,
    )
```

```python
import functools
import math

import jax
import jax.numpy as jnp
from jax import lax
from jax.experimental import pallas as pl
from jax.experimental.pallas import tpu as pltpu
from jax.sharding import PartitionSpec as P

MESH = pl.DeviceIdType.MESH
F32, BF16 = jnp.float32, jnp.bfloat16
UNIT = 64
EXT = 1152
N_SEND, N_RECV = 160, 160
ORDER = [
    "start", "own0", "z0s", "own1", "deq", "back", "d1", "rawdown", "x+0", "x-0", "g1", "own2", "deq2", "x+1",
    "x-1", "z0", "own3", "mv_own", "d2", "mi_own", "xf0", "y01_0", "d3", "x-2", "low", "h1", "x+2", "z-1",
    "own4", "low2", "g2", "z1", "p0", "y01_-1", "x+3", "x-3", "h2", "y01_1", "y0-1_1", "z2", "p-1", "y1-1_0",
    "x-4", "ss1", "mvs1", "mis1", "g3", "x+4", "ss-1", "yf_1", "y1-1_-1", "h3", "mvs-1", "mis-1", "y01_2",
    "so0", "ss2", "g4", "h4", "so-1", "mvo0", "mio0", "mvs2", "p2", "mis2", "mvo-1", "mio-1", "so1", "y1-1_2",
    "g5", "mvo1", "mio1", "g6", "so2", "mvo2", "mio2", "g7", "g8",
]
BY_PAIR = (1,)


def nn(a, b):
    return jnp.dot(a, b, preferred_element_type=F32)


def nt(a, b):
    return lax.dot_general(a, b, (((1,), (1,)), ((), ())), preferred_element_type=F32)


def kernel(
    limit,
    x_hbm, g_hbm, codes_hbm, scales_hbm, down_hbm, up_hbm,
    vout, ig, dgo, ugo,
    inp, cot, cod, scl, scf, upv, wt, dn, raw, g1, a2, b2, s2, a3, b3, s3, a4, b4,
    raw_u, g1_u, a2_u, b2_u, s2_u, a3_u, b3_u, s3_u, a4_u, b4_u, t5, e6, f7,
    vacc, back, back_t, low, low_t,
    load_sem, send_sem, recv_sem,
):
    rep, fs_me = lax.axis_index("rep"), lax.axis_index("fsdp")
    c = lax.rem(rep, 2)
    y = lax.rem(lax.div(rep, 2), 4)
    zl = lax.div(rep, 8)
    x = lax.div(fs_me, 2)
    zh = lax.rem(fs_me, 2)
    r = lax.rem(lax.rem(zl, 2) + lax.div(zl, 2), 2)
    zp = zl + 1 - 2 * lax.rem(zl, 2)

    def dev(dx=0, dy=0, zl_=zl, zh_=zh, c_=c):
        return {
            "rep": (zl_ * 4 + lax.rem(y + dy + 4, 4)) * 2 + c_,
            "fsdp": lax.rem(x + dx + 4, 4) * 2 + zh_,
        }

    sibling = dev(c_=1 - c)
    pair = dev(zl_=zp)
    mirror = dev(zl_=3 - zl, zh_=1 - zh)

    def same(dx):
        return lax.rem(x + dx + 4, 4) * 2 + zh

    def other(dx):
        return lax.rem(x + dx + 4, 4) * 2 + (1 - zh)

    names, sends = {}, []

    def sem(*key):
        return recv_sem.at[names.setdefault(key, len(names))]

    def send(ref, device, *key, dst=None):
        copy = pltpu.make_async_remote_copy(
            src_ref=ref,
            dst_ref=ref if dst is None else dst,
            send_sem=send_sem.at[len(sends)],
            recv_sem=sem(*key),
            device_id=device,
            device_id_type=MESH,
        )
        copy.start()
        sends.append(copy)

    def arrive(ref, *key):
        pltpu.make_async_copy(ref, ref, sem(*key)).wait()

    half = c * 512
    loads = {}

    def load(name, src, dst):
        loads[name] = pltpu.make_async_copy(src, dst, load_sem.at[len(loads)])
        loads[name].start()

    rows_mine, rows_sib = pl.ds(pl.multiple_of(half, 512), 512), pl.ds(pl.multiple_of(512 - half, 512), 512)
    load("scales", scales_hbm, scl)
    load("codes", codes_hbm.at[rows_mine], cod.at[rows_mine])
    load("down", down_hbm, dn.at[fs_me])
    load("up", up_hbm, upv)
    load("cot", g_hbm, cot)
    for f in range(8):
        load(("x", f), x_hbm.at[:, pl.ds(f * 1024, 1024)], inp.at[f])
    load("codes2", codes_hbm.at[rows_sib], cod.at[rows_sib])

    peers = [sibling, pair]
    peers += [dev(dx=d) for d in (1, 2, 3)]
    peers += [dev(dx=d, zl_=3 - zl, zh_=1 - zh) for d in range(4)]
    peers += [dev(dy=d) for d in (1, 2, 3)]
    peers += [dev(dy=d, zl_=3 - zl) for d in range(4)]
    barrier = pltpu.get_barrier_semaphore()
    for peer in peers:
        pl.semaphore_signal(barrier, inc=1, device_id=peer, device_id_type=MESH)

    def dequantize(block):
        rows = pl.ds(pl.multiple_of(block * UNIT, UNIT), UNIT)
        wt[fs_me, rows, :] = (cod[rows, :].astype(F32) * scf[pl.ds(block, 1), :]).astype(BF16)

    def unit(f, u, n=1):
        return wt.at[f, pl.ds(pl.multiple_of(half + u * UNIT, UNIT), n * UNIT)]

    u_me, u_pair = 2 * y + r, 2 * y + 1 - r

    def chunk(d):
        return 2 * lax.rem(y + d + 4, 4)

    pieces = [(u_me, 1), (u_pair, 1), (chunk(1), 2), (chunk(2), 2), (chunk(3), 2)]
    cols_mine = pl.ds(pl.multiple_of(half, 512), 512)
    cols_sib = pl.ds(pl.multiple_of(512 - half, 512), 512)

    def dpart(f, cols=cols_mine):
        return dn.at[f, :, cols]

    def x_send(m):
        for way in (1, -1):
            send(unit(fs_me, *pieces[m]), dev(dx=way), "x", way, m)


    def z_send(dx):
        send(unit(same(dx), u_me), mirror, "z", dx)

    def share(f, *key):
        send(wt.at[f, rows_mine], sibling, "c", *key)

    def values_term(f, first=False):
        term = nn(inp[f], wt[f])
        vacc[...] = term if first else vacc[...] + term

    def input_grad(f):
        ig[f] = (nt(cot[...], wt[f]) + nn(back[...], dn[f])).astype(BF16)

    steps = {}

    def step(name):
        def keep_it(fn):
            steps[name] = fn
            return fn

        return keep_it

    @step("start")
    def _():
        loads["scales"].wait()
        scf[...] = scl[...].astype(F32)
        loads["codes"].wait()
        dequantize(c * 8 + u_me)
        loads["down"].wait()
        pl.semaphore_wait(barrier, len(peers))
        for d in (1, 3, 2):
            send(dpart(fs_me), dev(dx=d), "d1", d)

    for m in range(5):
        steps[f"own{m}"] = functools.partial(x_send, m)
    steps["z0s"] = lambda: z_send(0)

    @step("own1")
    def _():
        dequantize(c * 8 + u_pair)
        x_send(1)

    @step("deq")
    def _():
        @pl.loop(1, 4)
        def _(d):
            for k in range(2):
                dequantize(c * 8 + 2 * lax.rem(y + d, 4) + k)

    @step("back")
    def _():
        loads["cot"].wait()
        loads["up"].wait()
        back[...] = (2.0 * nt(cot[...], upv[...])).astype(BF16)
        back_t[...] = (2.0 * nt(upv[...], cot[...])).astype(BF16)

    @step("rawdown")
    def _():
        for f in range(8):
            loads[("x", f)].wait()

        @pl.loop(0, 8)
        def _(f):
            raw[f] = nn(back_t[...], inp[f])

        send(raw.at[:, pl.ds(pl.multiple_of(32 - c * 32, 32), 32), :], sibling, "g1", dst=g1)

    @step("deq2")
    def _():
        loads["codes2"].wait()

        @pl.loop(0, 8)
        def _(k):
            dequantize((1 - c) * 8 + k)

    steps["mv_own"] = lambda: values_term(fs_me, first=True)
    steps["mi_own"] = lambda: input_grad(fs_me)

    @step("d1")
    def _():
        for d in (1, 3, 2):
            arrive(dpart(same(-d)), "d1", d)
        send(dpart(y * 2 + zh), mirror, "d2")
        for d in (1, 2, 3):
            send(dpart(same(-d)), sibling, "d4", d)

    @step("d2")
    def _():
        arrive(dpart(y * 2 + 1 - zh), "d2")
        for d in (1, 3, 2):
            send(dpart(y * 2 + 1 - zh), dev(dy=d), "d3", d)
        send(dpart(y * 2 + 1 - zh), sibling, "d4", 0)

    @step("d3")
    def _():
        for d in (1, 3, 2):
            arrive(dpart(lax.rem(y - d + 4, 4) * 2 + 1 - zh), "d3", d)
            send(dpart(lax.rem(y - d + 4, 4) * 2 + 1 - zh), sibling, "d4", 3 + d)

    @step("low")
    def _():
        for d in (1, 2, 3):
            arrive(dpart(same(-d), cols_sib), "d4", d)
        arrive(dpart(y * 2 + 1 - zh, cols_sib), "d4", 0)
        for d in (1, 2, 3):
            arrive(dpart(lax.rem(y - d + 4, 4) * 2 + 1 - zh, cols_sib), "d4", 3 + d)
        low_t[...] = jnp.zeros_like(low_t)

        @pl.loop(0, 8)
        def _(f):
            low_t[...] += nt(dn[f], inp[f])

        up_term = 2.0 * nn(low_t[...].astype(BF16), cot[...])
        for f in range(8):
            raw_u[f] = up_term[:, f * 128 : f * 128 + 128]
        send(raw_u.at[:, pl.ds(pl.multiple_of(32 - c * 32, 32), 32), :], sibling, "h1", dst=g1_u)

    @step("low2")
    def _():
        low[...] = jnp.zeros_like(low)

        @pl.loop(0, 8)
        def _(f):
            low[...] += nt(inp[f], dn[f])

    keep, give = pl.ds(pl.multiple_of(r * 16, 16), 16), pl.ds(pl.multiple_of(16 - r * 16, 16), 16)
    keep_c = pl.ds(pl.multiple_of(c * 32 + r * 16, 16), 16)
    give_c = pl.ds(pl.multiple_of(c * 32 + 16 - r * 16, 16), 16)

    def reduce_steps(g, raw, g1, a2, b2, s2, a3, b3, s3, a4, b4):
        @step(g + "1")
        def _():
            arrive(g1, g + "1")

            @pl.loop(0, 8)
            def _(f):
                a2[f] = (raw[f, give_c, :] + g1[f, give, :]).astype(BF16)
                s2[f] = raw[f, keep_c, :] + g1[f, keep, :]

            send(a2, pair, g + "2", dst=b2)

        @step(g + "2")
        def _():
            arrive(b2, g + "2")
            for k in range(4):
                a3[k] = (s2[k * 2 + 1 - zh] + b2[k * 2 + 1 - zh].astype(F32)).astype(BF16)
            send(a3, mirror, g + "3", dst=b3)
            for k in range(4):
                s3[k] = s2[k * 2 + zh] + b2[k * 2 + zh].astype(F32)

        @step(g + "3")
        def _():
            arrive(b3, g + "3")
            for d in (1, 3, 2):
                k = lax.rem(x + d, 4)
                a4[d - 1] = (s3[k] + b3[k].astype(F32)).astype(BF16)
                send(a4.at[d - 1], dev(dx=d), g + "4", d, dst=b4.at[d - 1])

        def total():
            t = s3[x] + b3[x].astype(F32)
            for d in (1, 2, 3):
                arrive(b4.at[d - 1], g + "4", d)
                t += b4[d - 1].astype(F32)
            return t

        return total

    total_down = reduce_steps("g", raw, g1, a2, b2, s2, a3, b3, s3, a4, b4)
    total_up = reduce_steps("h", raw_u, g1_u, a2_u, b2_u, s2_u, a3_u, b3_u, s3_u, a4_u, b4_u)
    mine = y * 2 + lax.div(zl, 2)
    q = c * 2 + r
    others = [(d, flip) for d in (1, 3, 0, 2) for flip in range(2) if d or flip]

    @step("g4")
    def _():
        t5[mine, :, 0:1024] = total_down().astype(BF16)

    @step("h4")
    def _():
        t5[mine, :, 1024:EXT] = total_up().astype(BF16)
        for d, flip in others:
            send(t5.at[mine], dev(dy=d, zl_=3 - zl if flip else zl), "g5", d, flip)

    @step("g5")
    def _():
        for d, flip in others:
            at = lax.rem(y - d + 4, 4) * 2 + (1 - lax.div(zl, 2) if flip else lax.div(zl, 2))
            arrive(t5.at[at], "g5", d, flip)
        total = t5[0].astype(F32)
        for k in range(1, 8):
            total += t5[k].astype(F32)
        square = total * total
        square = square[0:8] + square[8:16]
        tile = square[:, 0:128]
        for k in range(1, 9):
            tile += square[:, k * 128 : k * 128 + 128]
        e6[fs_me, 0:16, :] = total[:, 1024:EXT]
        e6[fs_me, 16:24, :] = tile
        for d, flip in others:
            device = dev(dx=d, zl_=3 - zl, zh_=1 - zh) if flip else dev(dx=d)
            send(e6.at[fs_me], device, "g6", d, flip)
        f7[q, 0:16, :] = total[:, 0:1024]

    @step("g6")
    def _():
        for d, flip in others:
            at = other(-d) if flip else same(-d)
            arrive(e6.at[at], "g6", d, flip)
        tile = e6[0, 16:24, :]
        for f in range(8):
            f7[q, 16:32, f * 128 : f * 128 + 128] = e6[f, 0:16, :]
            if f:
                tile += e6[f, 16:24, :]
        f7[q, 32:40, 0:128] = tile
        f7[q, 32:40, 128:1024] = jnp.zeros((8, 896), F32)
        send(f7.at[q], pair, "g7")

    @step("g7")
    def _():
        arrive(f7.at[c * 2 + 1 - r], "g7")
        send(f7.at[pl.ds(c * 2, 2)], sibling, "g8")

    @step("g8")
    def _():
        arrive(f7.at[pl.ds(2 - c * 2, 2)], "g8")
        tile = f7[0, 32:40, 0:128]
        for k in range(1, 4):
            tile += f7[k, 32:40, 0:128]
        squares = jnp.sum(jnp.sum(tile, axis=1, keepdims=True), axis=0, keepdims=True)
        factor = jnp.minimum(1.0, limit / jnp.sqrt(squares))
        for k in range(4):
            dgo[k * 16 : k * 16 + 16, :] = factor * f7[k, 0:16, :]
            ugo[k * 16 : k * 16 + 16, :] = factor * f7[k, 16:32, :]

    onward = {1: ((0, 0, 1), (2, 0, 2), (4, 0, 1)), -1: ((1, 0, 1), (3, 0, 2), (4, 1, 1))}

    def from_x(way, m):
        arrive(unit(same(-way), *pieces[m]), "x", way, m)
        for k, first, n in onward[way]:
            if k == m:
                send(unit(same(-way), pieces[m][0] + first, n), dev(dx=way), "xf", m, first)
        if m == 0:
            z_send(-way)

    def far_arrive(m, first, n):
        arrive(unit(same(2), pieces[m][0] + first, n), "xf", m, first)

    for m in range(5):
        steps[f"x+{m}"] = functools.partial(from_x, 1, m)
        steps[f"x-{m}"] = functools.partial(from_x, -1, m)

    @step("xf0")
    def _():
        far_arrive(0, 0, 1)
        z_send(2)

    @step("ss2")
    def _():
        for m, first, n in ((1, 0, 1), (2, 0, 2), (3, 0, 2), (4, 0, 1), (4, 1, 1)):
            far_arrive(m, first, n)
        share(same(2), "s", 2)

    def other_steps(dx, by_pair, way):
        f = other(dx)

        @step(f"z{dx}")
        def _():
            arrive(unit(f, u_me), "z", dx)
            if not by_pair:
                send(unit(f, u_me), pair, "p", dx)
            for w in (1, -1):
                send(unit(f, u_me), dev(dy=w), "y0", w, dx)
            if by_pair:
                send(unit(f, u_me), pair, "p", dx)

        if by_pair:
            for w in (1, -1):

                @step(f"y0{w}_{dx}")
                def _(w=w):
                    arrive(unit(f, chunk(-w) + r), "y0", w, dx)
                    if w == way:
                        send(unit(f, chunk(-w) + r), dev(dy=w), "yf", dx)
                    send(unit(f, chunk(-w) + r), pair, "pb", w, dx)

            @step(f"yf_{dx}")
            def _():
                arrive(unit(f, chunk(2) + r), "yf", dx)
                send(unit(f, chunk(2) + r), pair, "pb", 0, dx)

            @step(f"so{dx}")
            def _():
                arrive(unit(f, u_pair), "p", dx)
                for w, d in ((1, -1), (-1, 1), (0, 2)):
                    arrive(unit(f, chunk(d) + 1 - r), "pb", w, dx)
                share(f, "o", dx)

        else:

            @step(f"p{dx}")
            def _():
                arrive(unit(f, u_pair), "p", dx)
                for w in (1, -1):
                    send(unit(f, u_pair), dev(dy=w), "y1", w, dx)

            @step(f"y01_{dx}")
            def _():
                arrive(unit(f, chunk(-1) + r), "y0", 1, dx)
                send(unit(f, chunk(-1) + r), dev(dy=1), "yf0", dx)

            @step(f"y1-1_{dx}")
            def _():
                arrive(unit(f, chunk(1) + 1 - r), "y1", -1, dx)
                send(unit(f, chunk(1) + 1 - r), dev(dy=-1), "yf1", dx)

            @step(f"so{dx}")
            def _():
                arrive(unit(f, chunk(1) + r), "y0", -1, dx)
                arrive(unit(f, chunk(-1) + 1 - r), "y1", 1, dx)
                arrive(unit(f, chunk(2) + r), "yf0", dx)
                arrive(unit(f, chunk(2) + 1 - r), "yf1", dx)
                share(f, "o", dx)

    for dx in (0, -1, 1, 2):
        way = 1 if dx in BY_PAIR and BY_PAIR.index(dx) % 2 == 0 else -1
        other_steps(dx, dx in BY_PAIR, way)

    def to_values(kind, f, dx):
        arrive(wt.at[f, rows_sib], "c", kind, dx)
        values_term(f)

    for dx in (-1, 1, 2, 0):
        if dx:
            steps[f"mvs{dx}"] = functools.partial(to_values, "s", same(dx), dx)
            steps[f"mis{dx}"] = functools.partial(input_grad, same(dx))
        steps[f"mvo{dx}"] = functools.partial(to_values, "o", other(dx), dx)
        steps[f"mio{dx}"] = functools.partial(input_grad, other(dx))
    for dx in (-1, 1):
        steps[f"ss{dx}"] = functools.partial(share, same(dx), "s", dx)

    for name in ORDER:
        steps.pop(name)()
    assert not steps
    vout[...] = (vacc[...] + 2.0 * nn(low[...].astype(BF16), upv[...])).astype(BF16)
    for copy in sends:
        copy.wait_send()
    assert len(names) <= N_RECV and len(sends) <= N_SEND


def place(vout, ig, dgo, ugo, val_hbm, ig_hbm, dg_hbm, ug_hbm, sems):
    copies = [pltpu.make_async_copy(ig.at[f], ig_hbm.at[:, pl.ds(f * 1024, 1024)], sems.at[f]) for f in range(8)]
    for k, (src, dst) in enumerate(((vout, val_hbm), (dgo, dg_hbm), (ugo, ug_hbm))):
        copies.append(pltpu.make_async_copy(src, dst, sems.at[8 + k]))
    for copy in copies:
        copy.start()
    for copy in copies:
        copy.wait()


def local(*arguments):
    inputs, adapter_up = arguments[0], arguments[5]
    rank, values_width = adapter_up.shape
    limit = math.sqrt(rank * (inputs.shape[1] + values_width))
    scratch = [
        pltpu.VMEM((8, 256, 1024), BF16),
        pltpu.VMEM((256, 1024), BF16),
        pltpu.VMEM((1024, 1024), BF16),
        pltpu.VMEM((16, 1024), BF16),
        pltpu.VMEM((16, 1024), F32),
        pltpu.VMEM((64, 1024), BF16),
        pltpu.VMEM((8, 1024, 1024), BF16),
        pltpu.VMEM((8, 64, 1024), BF16),
        pltpu.VMEM((8, 64, 1024), F32),
        pltpu.VMEM((8, 32, 1024), F32),
        pltpu.VMEM((8, 16, 1024), BF16),
        pltpu.VMEM((8, 16, 1024), BF16),
        pltpu.VMEM((8, 16, 1024), F32),
        pltpu.VMEM((4, 16, 1024), BF16),
        pltpu.VMEM((4, 16, 1024), BF16),
        pltpu.VMEM((4, 16, 1024), F32),
        pltpu.VMEM((3, 16, 1024), BF16),
        pltpu.VMEM((3, 16, 1024), BF16),
        pltpu.VMEM((8, 64, 128), F32),
        pltpu.VMEM((8, 32, 128), F32),
        pltpu.VMEM((8, 16, 128), BF16),
        pltpu.VMEM((8, 16, 128), BF16),
        pltpu.VMEM((8, 16, 128), F32),
        pltpu.VMEM((4, 16, 128), BF16),
        pltpu.VMEM((4, 16, 128), BF16),
        pltpu.VMEM((4, 16, 128), F32),
        pltpu.VMEM((3, 16, 128), BF16),
        pltpu.VMEM((3, 16, 128), BF16),
        pltpu.VMEM((8, 16, EXT), BF16),
        pltpu.VMEM((8, 24, 128), F32),
        pltpu.VMEM((4, 40, 1024), F32),
        pltpu.VMEM((256, 1024), F32),
        pltpu.VMEM((256, 64), BF16),
        pltpu.VMEM((64, 256), BF16),
        pltpu.VMEM((256, 64), F32),
        pltpu.VMEM((64, 256), F32),
        pltpu.SemaphoreType.DMA((16,)),
        pltpu.SemaphoreType.DMA((N_SEND,)),
        pltpu.SemaphoreType.DMA((N_RECV,)),
    ]
    hbm = pl.BlockSpec(memory_space=pl.ANY)
    results = pl.pallas_call(
        functools.partial(kernel, limit),
        out_shape=(
            pltpu.VMEM((256, 1024), BF16),
            pltpu.VMEM((8, 256, 1024), BF16),
            pltpu.VMEM((64, 1024), F32),
            pltpu.VMEM((64, 1024), F32),
        ),
        in_specs=[hbm] * 6,
        out_specs=(pl.BlockSpec(memory_space=pltpu.VMEM),) * 4,
        scratch_shapes=scratch,
        cost_estimate=pl.CostEstimate(flops=9_600_000_000, bytes_accessed=12_000_000, transcendentals=0),
        compiler_params=pltpu.CompilerParams(
            collective_id=0, has_side_effects=True, vmem_limit_bytes=38 << 20
        ),
    )(*(pltpu.with_memory_space_constraint(a, pltpu.HBM) for a in arguments))
    return pl.pallas_call(
        place,
        out_shape=(
            jax.ShapeDtypeStruct((256, 1024), BF16),
            jax.ShapeDtypeStruct((256, 8192), BF16),
            jax.ShapeDtypeStruct((64, 1024), F32),
            jax.ShapeDtypeStruct((64, 1024), F32),
        ),
        in_specs=[pl.BlockSpec(memory_space=pltpu.VMEM)] * 4,
        out_specs=(hbm,) * 4,
        scratch_shapes=[pltpu.SemaphoreType.DMA((11,))],
        compiler_params=pltpu.CompilerParams(vmem_limit_bytes=1 << 20),
    )(*(pltpu.with_memory_space_constraint(a, pltpu.VMEM) for a in results))


def solution(mesh):
    return jax.shard_map(
        local,
        mesh=mesh,
        in_specs=(
            P(("rep", "fsdp"), None),
            P(("rep", "fsdp"), None),
            P("fsdp", None),
            P("fsdp", None),
            P(None, "fsdp"),
            P(),
        ),
        out_specs=(P(("rep", "fsdp"), None), P(("rep", "fsdp"), None), P(None, "fsdp"), P()),
        check_vma=False,
    )
```

```python
import functools
import math

import jax
import jax.numpy as jnp
from jax import lax
from jax.experimental import pallas as pl
from jax.experimental.pallas import tpu as pltpu
from jax.sharding import PartitionSpec as P

MESH = pl.DeviceIdType.MESH
F32, BF16 = jnp.float32, jnp.bfloat16
UNIT = 64
EXT = 1152
N_SEND, N_RECV = 224, 224
ORDER = [
    "start", "own0", "z0s", "own1", "deq", "back", "rawdown", "g1", "d2", "own3", "own2", "x-0", "d1", "x+0",
    "deq2", "x-1", "own4", "x+1", "mv_own", "z0", "mi_own", "d3", "g2", "low", "h1", "low2", "z1", "y01_0",
    "x+3", "x-3", "p0", "y01_1", "z-1", "x+2", "x-2", "h2", "y1-1_0", "xf0", "g3", "p1", "y01_-1", "p-1",
    "h3", "xo", "so0", "x-4", "ss1", "x+4", "ss-1", "mvo0", "mio0", "y1-1_1", "z2", "mvs1", "mis1", "y1-1_-1",
    "mvs-1", "mis-1", "g4", "h4", "p2", "y01_2", "g5", "so-1", "so1", "y1-1_2", "mvo-1", "mio-1", "ss2",
    "mvo1", "g6", "mio1", "mvs2", "so2", "mis2", "g7", "mvo2", "mio2", "g8",
]
BY_PAIR = ()
PARTS = {}
FINE = (0, -1, 1, 2)


def nn(a, b):
    return jnp.dot(a, b, preferred_element_type=F32)


def nt(a, b):
    return lax.dot_general(a, b, (((1,), (1,)), ((), ())), preferred_element_type=F32)


def kernel(
    limit,
    x_hbm, g_hbm, codes_hbm, scales_hbm, down_hbm, up_hbm,
    vout, ig, dgo, ugo,
    inp, cot, cod, scl, scf, upv, wt, dn, raw, g1, a2, b2, s2, a3, b3, s3, a4, b4,
    raw_u, g1_u, a2_u, b2_u, s2_u, a3_u, b3_u, s3_u, a4_u, b4_u, t5, e6, f7,
    vacc, back, back_t, low, low_t,
    load_sem, send_sem, recv_sem,
):
    rep, fs_me = lax.axis_index("rep"), lax.axis_index("fsdp")
    c = lax.rem(rep, 2)
    y = lax.rem(lax.div(rep, 2), 4)
    zl = lax.div(rep, 8)
    x = lax.div(fs_me, 2)
    zh = lax.rem(fs_me, 2)
    r = lax.rem(lax.rem(zl, 2) + lax.div(zl, 2), 2)
    zp = zl + 1 - 2 * lax.rem(zl, 2)

    def dev(dx=0, dy=0, zl_=zl, zh_=zh, c_=c):
        return {
            "rep": (zl_ * 4 + lax.rem(y + dy + 4, 4)) * 2 + c_,
            "fsdp": lax.rem(x + dx + 4, 4) * 2 + zh_,
        }

    sibling = dev(c_=1 - c)
    pair = dev(zl_=zp)
    mirror = dev(zl_=3 - zl, zh_=1 - zh)

    def same(dx):
        return lax.rem(x + dx + 4, 4) * 2 + zh

    def other(dx):
        return lax.rem(x + dx + 4, 4) * 2 + (1 - zh)

    names, sends = {}, []

    def sem(*key):
        return recv_sem.at[names.setdefault(key, len(names))]

    def send(ref, device, *key, dst=None):
        copy = pltpu.make_async_remote_copy(
            src_ref=ref,
            dst_ref=ref if dst is None else dst,
            send_sem=send_sem.at[len(sends)],
            recv_sem=sem(*key),
            device_id=device,
            device_id_type=MESH,
        )
        copy.start()
        sends.append(copy)

    def arrive(ref, *key):
        pltpu.make_async_copy(ref, ref, sem(*key)).wait()

    half = c * 512
    loads = {}

    def load(name, src, dst):
        loads[name] = pltpu.make_async_copy(src, dst, load_sem.at[len(loads)])
        loads[name].start()

    rows_mine, rows_sib = pl.ds(pl.multiple_of(half, 512), 512), pl.ds(pl.multiple_of(512 - half, 512), 512)
    load("scales", scales_hbm, scl)
    load("codes", codes_hbm.at[rows_mine], cod.at[rows_mine])
    load("down", down_hbm, dn.at[fs_me])
    load("up", up_hbm, upv)
    load("cot", g_hbm, cot)
    for f in range(8):
        load(("x", f), x_hbm.at[:, pl.ds(f * 1024, 1024)], inp.at[f])
    load("codes2", codes_hbm.at[rows_sib], cod.at[rows_sib])

    peers = [sibling, pair]
    peers += [dev(dx=d) for d in (1, 2, 3)]
    peers += [dev(dx=d, zl_=3 - zl, zh_=1 - zh) for d in range(4)]
    peers += [dev(dy=d) for d in (1, 2, 3)]
    peers += [dev(dy=d, zl_=3 - zl) for d in range(4)]
    barrier = pltpu.get_barrier_semaphore()
    for peer in peers:
        pl.semaphore_signal(barrier, inc=1, device_id=peer, device_id_type=MESH)

    def dequantize(block):
        rows = pl.ds(pl.multiple_of(block * UNIT, UNIT), UNIT)
        wt[fs_me, rows, :] = (cod[rows, :].astype(F32) * scf[pl.ds(block, 1), :]).astype(BF16)

    def unit(f, u, n=1, base=half):
        return wt.at[f, pl.ds(pl.multiple_of(base + u * UNIT, UNIT), n * UNIT)]

    def part(f, u, k, dx, base=half):
        rows = UNIT // PARTS.get(dx, 1)
        return wt.at[f, pl.ds(pl.multiple_of(base + u * UNIT + k * rows, rows), rows)]

    u_me, u_pair = 2 * y + r, 2 * y + 1 - r

    def chunk(d):
        return 2 * lax.rem(y + d + 4, 4)

    pieces = [(u_me, 1), (u_pair, 1), (chunk(1), 2), (chunk(2), 2), (chunk(3), 2)]
    cols_mine = pl.ds(pl.multiple_of(half, 512), 512)
    cols_sib = pl.ds(pl.multiple_of(512 - half, 512), 512)

    def dpart(f, cols=cols_mine):
        return dn.at[f, :, cols]

    def x_send(m):
        for way in (1, -1):
            send(unit(fs_me, *pieces[m]), dev(dx=way), "x", way, m)


    def z_send(dx):
        for k in range(PARTS.get(dx, 1)):
            send(part(same(dx), u_me, k, dx), mirror, "z", dx, k)

    def share(f, *key):
        send(wt.at[f, rows_mine], sibling, "c", *key)

    def values_term(f, first=False):
        term = nn(inp[f], wt[f])
        vacc[...] = term if first else vacc[...] + term

    def input_grad(f):
        ig[f] = (nt(cot[...], wt[f]) + nn(back[...], dn[f])).astype(BF16)

    steps = {}

    def step(name):
        def keep_it(fn):
            steps[name] = fn
            return fn

        return keep_it

    @step("start")
    def _():
        loads["scales"].wait()
        scf[...] = scl[...].astype(F32)
        loads["codes"].wait()
        dequantize(c * 8 + u_me)
        loads["down"].wait()
        pl.semaphore_wait(barrier, len(peers))
        for d in (1, 3, 2):
            send(dpart(fs_me), dev(dx=d), "d1", d)
        send(dpart(fs_me), mirror, "d2")

    for m in range(5):
        steps[f"own{m}"] = functools.partial(x_send, m)
    steps["z0s"] = lambda: z_send(0)

    @step("own1")
    def _():
        dequantize(c * 8 + u_pair)
        x_send(1)

    @step("deq")
    def _():
        @pl.loop(1, 4)
        def _(d):
            for k in range(2):
                dequantize(c * 8 + 2 * lax.rem(y + d, 4) + k)

    @step("back")
    def _():
        loads["cot"].wait()
        loads["up"].wait()
        back[...] = (2.0 * nt(cot[...], upv[...])).astype(BF16)
        back_t[...] = (2.0 * nt(upv[...], cot[...])).astype(BF16)

    @step("rawdown")
    def _():
        for f in range(8):
            loads[("x", f)].wait()

        @pl.loop(0, 8)
        def _(f):
            raw[f] = nn(back_t[...], inp[f])

        send(raw.at[:, pl.ds(pl.multiple_of(32 - c * 32, 32), 32), :], sibling, "g1", dst=g1)

    @step("deq2")
    def _():
        loads["codes2"].wait()

        @pl.loop(0, 8)
        def _(k):
            dequantize((1 - c) * 8 + k)

    steps["mv_own"] = lambda: values_term(fs_me, first=True)
    steps["mi_own"] = lambda: input_grad(fs_me)

    @step("d1")
    def _():
        for d in (1, 3, 2):
            arrive(dpart(same(-d)), "d1", d)
        for d in (1, 2, 3):
            send(dpart(same(-d)), sibling, "d4", d)

    @step("d2")
    def _():
        arrive(dpart(other(0)), "d2")
        for d in (1, 3, 2):
            send(dpart(other(0)), dev(dx=d), "d3", d)
        send(dpart(other(0)), sibling, "d4", 0)

    @step("d3")
    def _():
        for d in (1, 3, 2):
            arrive(dpart(other(-d)), "d3", d)
            send(dpart(other(-d)), sibling, "d4", 3 + d)

    @step("low")
    def _():
        for d in (1, 2, 3):
            arrive(dpart(same(-d), cols_sib), "d4", d)
        arrive(dpart(other(0), cols_sib), "d4", 0)
        for d in (1, 2, 3):
            arrive(dpart(other(-d), cols_sib), "d4", 3 + d)
        low_t[...] = jnp.zeros_like(low_t)

        @pl.loop(0, 8)
        def _(f):
            low_t[...] += nt(dn[f], inp[f])

        up_term = 2.0 * nn(low_t[...].astype(BF16), cot[...])
        for f in range(8):
            raw_u[f] = up_term[:, f * 128 : f * 128 + 128]
        send(raw_u.at[:, pl.ds(pl.multiple_of(32 - c * 32, 32), 32), :], sibling, "h1", dst=g1_u)

    @step("low2")
    def _():
        low[...] = jnp.zeros_like(low)

        @pl.loop(0, 8)
        def _(f):
            low[...] += nt(inp[f], dn[f])

    keep, give = pl.ds(pl.multiple_of(r * 16, 16), 16), pl.ds(pl.multiple_of(16 - r * 16, 16), 16)
    keep_c = pl.ds(pl.multiple_of(c * 32 + r * 16, 16), 16)
    give_c = pl.ds(pl.multiple_of(c * 32 + 16 - r * 16, 16), 16)

    def reduce_steps(g, raw, g1, a2, b2, s2, a3, b3, s3, a4, b4):
        @step(g + "1")
        def _():
            arrive(g1, g + "1")

            @pl.loop(0, 8)
            def _(f):
                a2[f] = (raw[f, give_c, :] + g1[f, give, :]).astype(BF16)
                s2[f] = raw[f, keep_c, :] + g1[f, keep, :]

            send(a2, pair, g + "2", dst=b2)

        @step(g + "2")
        def _():
            arrive(b2, g + "2")
            for k in range(4):
                a3[k] = (s2[k * 2 + 1 - zh] + b2[k * 2 + 1 - zh].astype(F32)).astype(BF16)
            send(a3, mirror, g + "3", dst=b3)
            for k in range(4):
                s3[k] = s2[k * 2 + zh] + b2[k * 2 + zh].astype(F32)

        @step(g + "3")
        def _():
            arrive(b3, g + "3")
            for d in (1, 3, 2):
                k = lax.rem(x + d, 4)
                a4[d - 1] = (s3[k] + b3[k].astype(F32)).astype(BF16)
                send(a4.at[d - 1], dev(dx=d), g + "4", d, dst=b4.at[d - 1])

        def total():
            t = s3[x] + b3[x].astype(F32)
            for d in (1, 2, 3):
                arrive(b4.at[d - 1], g + "4", d)
                t += b4[d - 1].astype(F32)
            return t

        return total

    total_down = reduce_steps("g", raw, g1, a2, b2, s2, a3, b3, s3, a4, b4)
    total_up = reduce_steps("h", raw_u, g1_u, a2_u, b2_u, s2_u, a3_u, b3_u, s3_u, a4_u, b4_u)
    mine = y * 2 + lax.div(zl, 2)
    q = c * 2 + r
    others = [(d, flip) for d in (1, 3, 0, 2) for flip in range(2) if d or flip]

    @step("g4")
    def _():
        t5[mine, :, 0:1024] = total_down().astype(BF16)

    @step("h4")
    def _():
        t5[mine, :, 1024:EXT] = total_up().astype(BF16)
        for d, flip in others:
            send(t5.at[mine], dev(dy=d, zl_=3 - zl if flip else zl), "g5", d, flip)

    @step("g5")
    def _():
        for d, flip in others:
            at = lax.rem(y - d + 4, 4) * 2 + (1 - lax.div(zl, 2) if flip else lax.div(zl, 2))
            arrive(t5.at[at], "g5", d, flip)
        total = t5[0].astype(F32)
        for k in range(1, 8):
            total += t5[k].astype(F32)
        square = total * total
        square = square[0:8] + square[8:16]
        tile = square[:, 0:128]
        for k in range(1, 9):
            tile += square[:, k * 128 : k * 128 + 128]
        e6[fs_me, 0:16, :] = total[:, 1024:EXT]
        e6[fs_me, 16:24, :] = tile
        for d, flip in others:
            device = dev(dx=d, zl_=3 - zl, zh_=1 - zh) if flip else dev(dx=d)
            send(e6.at[fs_me], device, "g6", d, flip)
        f7[q, 0:16, :] = total[:, 0:1024]
        send(f7.at[q, 0:16], pair, "g7", 0)

    @step("g6")
    def _():
        for d, flip in others:
            at = other(-d) if flip else same(-d)
            arrive(e6.at[at], "g6", d, flip)
        tile = e6[0, 16:24, :]
        for f in range(8):
            f7[q, 16:32, f * 128 : f * 128 + 128] = e6[f, 0:16, :]
            if f:
                tile += e6[f, 16:24, :]
        f7[q, 32:40, 0:128] = tile
        f7[q, 32:40, 128:1024] = jnp.zeros((8, 896), F32)
        send(f7.at[q, 16:40], pair, "g7", 1)

    @step("g7")
    def _():
        arrive(f7.at[c * 2 + 1 - r, 0:16], "g7", 0)
        arrive(f7.at[c * 2 + 1 - r, 16:40], "g7", 1)
        send(f7.at[pl.ds(c * 2, 2)], sibling, "g8")

    @step("g8")
    def _():
        arrive(f7.at[pl.ds(2 - c * 2, 2)], "g8")
        tile = f7[0, 32:40, 0:128]
        for k in range(1, 4):
            tile += f7[k, 32:40, 0:128]
        squares = jnp.sum(jnp.sum(tile, axis=1, keepdims=True), axis=0, keepdims=True)
        factor = jnp.minimum(1.0, limit / jnp.sqrt(squares))
        for k in range(4):
            dgo[k * 16 : k * 16 + 16, :] = factor * f7[k, 0:16, :]
            ugo[k * 16 : k * 16 + 16, :] = factor * f7[k, 16:32, :]

    onward = {1: ((0, 0, 1), (2, 0, 2), (4, 0, 1)), -1: ((1, 0, 1), (3, 0, 2), (4, 1, 1))}

    def from_x(way, m):
        arrive(unit(same(-way), *pieces[m]), "x", way, m)
        for k, first, n in onward[way]:
            if k == m:
                send(unit(same(-way), pieces[m][0] + first, n), dev(dx=way), "xf", m, first)
        if m == 0:
            z_send(-way)

    def far_arrive(m, first, n):
        arrive(unit(same(2), pieces[m][0] + first, n), "xf", m, first)

    for m in range(5):
        steps[f"x+{m}"] = functools.partial(from_x, 1, m)
        steps[f"x-{m}"] = functools.partial(from_x, -1, m)

    @step("xf0")
    def _():
        far_arrive(0, 0, 1)
        z_send(2)

    @step("ss2")
    def _():
        for m, first, n in ((1, 0, 1), (2, 0, 2), (3, 0, 2), (4, 0, 1), (4, 1, 1)):
            far_arrive(m, first, n)
        share(same(2), "s", 2)

    fine = {dx: [] for dx in FINE}

    def other_steps(dx, by_pair, way, p):
        f, n_parts = other(dx), PARTS.get(dx, 1)
        q = f"{dx}" if n_parts == 1 else f"{dx}{'ab'[p]}"

        def piece(u):
            return part(f, u, p, dx)

        def take(u, *key):
            arrive(piece(u), *key)
            if dx in fine:
                send(piece(u), sibling, "f", dx, len(fine[dx]))
                fine[dx].append((u, p))

        @step(f"z{q}")
        def _():
            arrive(piece(u_me), "z", dx, p)
            if not by_pair:
                send(piece(u_me), pair, "p", dx, p)
            for w in (1, -1):
                send(piece(u_me), dev(dy=w), "y0", w, dx, p)
            if by_pair:
                send(piece(u_me), pair, "p", dx, p)
            if dx in fine:
                send(piece(u_me), sibling, "f", dx, len(fine[dx]))
                fine[dx].append((u_me, p))

        if by_pair:
            for w in (1, -1):

                @step(f"y0{w}_{q}")
                def _(w=w):
                    arrive(piece(chunk(-w) + r), "y0", w, dx, p)
                    if w == way:
                        send(piece(chunk(-w) + r), dev(dy=w), "yf", dx, p)
                    send(piece(chunk(-w) + r), pair, "pb", w, dx, p)
                    if dx in fine:
                        send(piece(chunk(-w) + r), sibling, "f", dx, len(fine[dx]))
                        fine[dx].append((chunk(-w) + r, p))

            @step(f"yf_{q}")
            def _():
                arrive(piece(chunk(2) + r), "yf", dx, p)
                send(piece(chunk(2) + r), pair, "pb", 0, dx, p)
                if dx in fine:
                    send(piece(chunk(2) + r), sibling, "f", dx, len(fine[dx]))
                    fine[dx].append((chunk(2) + r, p))

            def rest():
                take(u_pair, "p", dx, p)
                for w, d in ((1, -1), (-1, 1), (0, 2)):
                    take(chunk(d) + 1 - r, "pb", w, dx, p)

        else:

            @step(f"p{q}")
            def _():
                arrive(piece(u_pair), "p", dx, p)
                for w in (1, -1):
                    send(piece(u_pair), dev(dy=w), "y1", w, dx, p)
                if dx in fine:
                    send(piece(u_pair), sibling, "f", dx, len(fine[dx]))
                    fine[dx].append((u_pair, p))

            @step(f"y01_{q}")
            def _():
                arrive(piece(chunk(-1) + r), "y0", 1, dx, p)
                if dx in (0, 2):
                    send(piece(chunk(-1) + r), dev(dy=1), "yf0", dx, p)
                if dx in fine:
                    send(piece(chunk(-1) + r), sibling, "f", dx, len(fine[dx]))
                    fine[dx].append((chunk(-1) + r, p))

            @step(f"y1-1_{q}")
            def _():
                arrive(piece(chunk(1) + 1 - r), "y1", -1, dx, p)
                if dx in (0, 2):
                    send(piece(chunk(1) + 1 - r), dev(dy=-1), "yf1", dx, p)
                if dx in fine:
                    send(piece(chunk(1) + 1 - r), sibling, "f", dx, len(fine[dx]))
                    fine[dx].append((chunk(1) + 1 - r, p))

            def rest():
                take(chunk(1) + r, "y0", -1, dx, p)
                take(chunk(-1) + 1 - r, "y1", 1, dx, p)
                if dx == 2:
                    take(chunk(2) + r, "yf0", dx, p)
                    take(chunk(2) + 1 - r, "yf1", dx, p)

        return rest

    @step("xo")
    def _():
        for p in range(PARTS.get(0, 1)):
            arrive(part(other(0), chunk(2) + r, p, 0), "yf0", 0, p)
            arrive(part(other(0), chunk(2) + 1 - r, p, 0), "yf1", 0, p)
        for way in (1, -1):
            send(unit(other(0), chunk(2), 2), dev(dx=way), "xo", way)

    def last_pieces(dx, rests):
        for rest in rests:
            rest()
        if dx in (1, -1):
            arrive(unit(other(dx), chunk(2), 2), "xo", -dx)
            if dx in fine:
                send(unit(other(dx), chunk(2), 2), sibling, "f", dx, "xo")
        if dx == 0 and dx in fine:
            send(unit(other(0), chunk(2), 2), sibling, "f", dx, "xo")
        if dx not in fine:
            share(other(dx), "o", dx)

    for dx in (0, -1, 1, 2):
        way = 1 if dx in BY_PAIR and BY_PAIR.index(dx) % 2 == 0 else -1
        rests = [other_steps(dx, dx in BY_PAIR, way, p) for p in range(PARTS.get(dx, 1))]
        steps[f"so{dx}"] = functools.partial(last_pieces, dx, rests)

    def to_values(kind, f, dx):
        if kind == "o" and dx in fine:
            for k, (u, p) in enumerate(fine[dx]):
                arrive(part(f, u, p, dx, 512 - half), "f", dx, k)
            if dx != 2:
                arrive(unit(f, chunk(2), 2, 512 - half), "f", dx, "xo")
        else:
            arrive(wt.at[f, rows_sib], "c", kind, dx)
        values_term(f)

    for dx in (-1, 1, 2, 0):
        if dx:
            steps[f"mvs{dx}"] = functools.partial(to_values, "s", same(dx), dx)
            steps[f"mis{dx}"] = functools.partial(input_grad, same(dx))
        steps[f"mvo{dx}"] = functools.partial(to_values, "o", other(dx), dx)
        steps[f"mio{dx}"] = functools.partial(input_grad, other(dx))
    for dx in (-1, 1):
        steps[f"ss{dx}"] = functools.partial(share, same(dx), "s", dx)

    for name in ORDER:
        steps.pop(name)()
    assert not steps
    vout[...] = (vacc[...] + 2.0 * nn(low[...].astype(BF16), upv[...])).astype(BF16)
    for copy in sends:
        copy.wait_send()
    assert len(names) <= N_RECV and len(sends) <= N_SEND


def place(vout, ig, dgo, ugo, val_hbm, ig_hbm, dg_hbm, ug_hbm, sems):
    copies = [pltpu.make_async_copy(ig.at[f], ig_hbm.at[:, pl.ds(f * 1024, 1024)], sems.at[f]) for f in range(8)]
    for k, (src, dst) in enumerate(((vout, val_hbm), (dgo, dg_hbm), (ugo, ug_hbm))):
        copies.append(pltpu.make_async_copy(src, dst, sems.at[8 + k]))
    for copy in copies:
        copy.start()
    for copy in copies:
        copy.wait()


def local(*arguments):
    inputs, adapter_up = arguments[0], arguments[5]
    rank, values_width = adapter_up.shape
    limit = math.sqrt(rank * (inputs.shape[1] + values_width))
    scratch = [
        pltpu.VMEM((8, 256, 1024), BF16),
        pltpu.VMEM((256, 1024), BF16),
        pltpu.VMEM((1024, 1024), BF16),
        pltpu.VMEM((16, 1024), BF16),
        pltpu.VMEM((16, 1024), F32),
        pltpu.VMEM((64, 1024), BF16),
        pltpu.VMEM((8, 1024, 1024), BF16),
        pltpu.VMEM((8, 64, 1024), BF16),
        pltpu.VMEM((8, 64, 1024), F32),
        pltpu.VMEM((8, 32, 1024), F32),
        pltpu.VMEM((8, 16, 1024), BF16),
        pltpu.VMEM((8, 16, 1024), BF16),
        pltpu.VMEM((8, 16, 1024), F32),
        pltpu.VMEM((4, 16, 1024), BF16),
        pltpu.VMEM((4, 16, 1024), BF16),
        pltpu.VMEM((4, 16, 1024), F32),
        pltpu.VMEM((3, 16, 1024), BF16),
        pltpu.VMEM((3, 16, 1024), BF16),
        pltpu.VMEM((8, 64, 128), F32),
        pltpu.VMEM((8, 32, 128), F32),
        pltpu.VMEM((8, 16, 128), BF16),
        pltpu.VMEM((8, 16, 128), BF16),
        pltpu.VMEM((8, 16, 128), F32),
        pltpu.VMEM((4, 16, 128), BF16),
        pltpu.VMEM((4, 16, 128), BF16),
        pltpu.VMEM((4, 16, 128), F32),
        pltpu.VMEM((3, 16, 128), BF16),
        pltpu.VMEM((3, 16, 128), BF16),
        pltpu.VMEM((8, 16, EXT), BF16),
        pltpu.VMEM((8, 24, 128), F32),
        pltpu.VMEM((4, 40, 1024), F32),
        pltpu.VMEM((256, 1024), F32),
        pltpu.VMEM((256, 64), BF16),
        pltpu.VMEM((64, 256), BF16),
        pltpu.VMEM((256, 64), F32),
        pltpu.VMEM((64, 256), F32),
        pltpu.SemaphoreType.DMA((16,)),
        pltpu.SemaphoreType.DMA((N_SEND,)),
        pltpu.SemaphoreType.DMA((N_RECV,)),
    ]
    hbm = pl.BlockSpec(memory_space=pl.ANY)
    results = pl.pallas_call(
        functools.partial(kernel, limit),
        out_shape=(
            pltpu.VMEM((256, 1024), BF16),
            pltpu.VMEM((8, 256, 1024), BF16),
            pltpu.VMEM((64, 1024), F32),
            pltpu.VMEM((64, 1024), F32),
        ),
        in_specs=[hbm] * 6,
        out_specs=(pl.BlockSpec(memory_space=pltpu.VMEM),) * 4,
        scratch_shapes=scratch,
        cost_estimate=pl.CostEstimate(flops=9_600_000_000, bytes_accessed=12_000_000, transcendentals=0),
        compiler_params=pltpu.CompilerParams(
            collective_id=0, has_side_effects=True, vmem_limit_bytes=38 << 20
        ),
    )(*(pltpu.with_memory_space_constraint(a, pltpu.HBM) for a in arguments))
    return pl.pallas_call(
        place,
        out_shape=(
            jax.ShapeDtypeStruct((256, 1024), BF16),
            jax.ShapeDtypeStruct((256, 8192), BF16),
            jax.ShapeDtypeStruct((64, 1024), F32),
            jax.ShapeDtypeStruct((64, 1024), F32),
        ),
        in_specs=[pl.BlockSpec(memory_space=pltpu.VMEM)] * 4,
        out_specs=(hbm,) * 4,
        scratch_shapes=[pltpu.SemaphoreType.DMA((11,))],
        compiler_params=pltpu.CompilerParams(vmem_limit_bytes=1 << 20),
    )(*(pltpu.with_memory_space_constraint(a, pltpu.VMEM) for a in results))


def solution(mesh):
    return jax.shard_map(
        local,
        mesh=mesh,
        in_specs=(
            P(("rep", "fsdp"), None),
            P(("rep", "fsdp"), None),
            P("fsdp", None),
            P("fsdp", None),
            P(None, "fsdp"),
            P(),
        ),
        out_specs=(P(("rep", "fsdp"), None), P(("rep", "fsdp"), None), P(None, "fsdp"), P()),
        check_vma=False,
    )
```

```python
import functools
import math

import jax
import jax.numpy as jnp
from jax import lax
from jax.experimental import pallas as pl
from jax.experimental.pallas import tpu as pltpu
from jax.sharding import PartitionSpec as P

MESH = pl.DeviceIdType.MESH
F32, BF16 = jnp.float32, jnp.bfloat16
UNIT = 64
EXT = 1152
N_SEND, N_RECV = 224, 224
ORDER = [
    "start", "own0", "z0s", "own1", "deq", "back", "rawdown", "g1", "d2", "own3", "own2", "x-0", "d1", "x+0",
    "deq2", "x-1", "own4", "x+1", "mv_own", "z0", "mi_own", "d3", "g2", "low", "h1", "low2", "z1", "y01_0",
    "x+3", "x-3", "p0", "y01_1", "z-1", "x+2", "x-2", "h2", "y1-1_0", "xf0", "g3", "p1", "y01_-1", "p-1",
    "h3", "xo", "so0", "x-4", "ss1", "x+4", "ss-1", "mvo0", "mio0", "y1-1_1", "z2", "mvs1", "mis1", "y1-1_-1",
    "mvs-1", "mis-1", "g4", "h4", "p2", "y01_2", "g5", "so-1", "so1", "y1-1_2", "mvo-1", "mio-1", "ss2",
    "mvo1", "g6", "mio1", "mvs2", "so2", "mis2", "g7", "mvo2", "mio2", "g8",
]
BY_PAIR = ()
PARTS = {}
FINE = (0, -1, 1, 2)


def nn(a, b):
    return jnp.dot(a, b, preferred_element_type=F32)


def nt(a, b):
    return lax.dot_general(a, b, (((1,), (1,)), ((), ())), preferred_element_type=F32)


def kernel(
    limit,
    x_hbm, g_hbm, codes_hbm, scales_hbm, down_hbm, up_hbm,
    vout, ig, dgo, ugo,
    inp, cot, cod, scl, scf, upv, wt, dn, raw, g1, a2, b2, s2, a3, b3, s3, a4, b4,
    raw_u, g1_u, a2_u, b2_u, s2_u, a3_u, b3_u, s3_u, a4_u, b4_u, t5, e6, f7,
    vacc, back, back_t, low, low_t,
    load_sem, send_sem, recv_sem,
):
    rep, fs_me = lax.axis_index("rep"), lax.axis_index("fsdp")
    c = lax.rem(rep, 2)
    y = lax.rem(lax.div(rep, 2), 4)
    zl = lax.div(rep, 8)
    x = lax.div(fs_me, 2)
    zh = lax.rem(fs_me, 2)
    r = lax.rem(lax.rem(zl, 2) + lax.div(zl, 2), 2)
    zp = zl + 1 - 2 * lax.rem(zl, 2)

    def dev(dx=0, dy=0, zl_=zl, zh_=zh, c_=c):
        return {
            "rep": (zl_ * 4 + lax.rem(y + dy + 4, 4)) * 2 + c_,
            "fsdp": lax.rem(x + dx + 4, 4) * 2 + zh_,
        }

    sibling = dev(c_=1 - c)
    pair = dev(zl_=zp)
    mirror = dev(zl_=3 - zl, zh_=1 - zh)

    def same(dx):
        return lax.rem(x + dx + 4, 4) * 2 + zh

    def other(dx):
        return lax.rem(x + dx + 4, 4) * 2 + (1 - zh)

    names, sends = {}, []

    def sem(*key):
        return recv_sem.at[names.setdefault(key, len(names))]

    def send(ref, device, *key, dst=None):
        copy = pltpu.make_async_remote_copy(
            src_ref=ref,
            dst_ref=ref if dst is None else dst,
            send_sem=send_sem.at[len(sends)],
            recv_sem=sem(*key),
            device_id=device,
            device_id_type=MESH,
        )
        copy.start()
        sends.append(copy)

    def arrive(ref, *key):
        pltpu.make_async_copy(ref, ref, sem(*key)).wait()

    peers = [sibling, pair]
    peers += [dev(dx=d) for d in (1, 2, 3)]
    peers += [dev(dx=d, zl_=3 - zl, zh_=1 - zh) for d in range(4)]
    peers += [dev(dy=d) for d in (1, 2, 3)]
    peers += [dev(dy=d, zl_=3 - zl) for d in range(4)]
    barrier = pltpu.get_barrier_semaphore()
    for peer in peers:
        pl.semaphore_signal(barrier, inc=1, device_id=peer, device_id_type=MESH)

    half = c * 512
    loads = {}

    def load(name, src, dst):
        loads[name] = pltpu.make_async_copy(src, dst, load_sem.at[len(loads)])
        loads[name].start()

    rows_mine, rows_sib = pl.ds(pl.multiple_of(half, 512), 512), pl.ds(pl.multiple_of(512 - half, 512), 512)
    load("scales", scales_hbm, scl)
    load("codes", codes_hbm.at[rows_mine], cod.at[rows_mine])
    load("down", down_hbm, dn.at[fs_me])
    load("up", up_hbm, upv)
    load("cot", g_hbm, cot)
    for f in range(8):
        load(("x", f), x_hbm.at[:, pl.ds(f * 1024, 1024)], inp.at[f])
    load("codes2", codes_hbm.at[rows_sib], cod.at[rows_sib])

    def dequantize(block):
        rows = pl.ds(pl.multiple_of(block * UNIT, UNIT), UNIT)
        wt[fs_me, rows, :] = (cod[rows, :].astype(F32) * scf[pl.ds(block, 1), :]).astype(BF16)

    def unit(f, u, n=1, base=half):
        return wt.at[f, pl.ds(pl.multiple_of(base + u * UNIT, UNIT), n * UNIT)]

    def part(f, u, k, dx, base=half):
        rows = UNIT // PARTS.get(dx, 1)
        return wt.at[f, pl.ds(pl.multiple_of(base + u * UNIT + k * rows, rows), rows)]

    u_me, u_pair = 2 * y + r, 2 * y + 1 - r

    def chunk(d):
        return 2 * lax.rem(y + d + 4, 4)

    pieces = [(u_me, 1), (u_pair, 1), (chunk(1), 2), (chunk(2), 2), (chunk(3), 2)]
    cols_mine = pl.ds(pl.multiple_of(half, 512), 512)
    cols_sib = pl.ds(pl.multiple_of(512 - half, 512), 512)

    def dpart(f, cols=cols_mine):
        return dn.at[f, :, cols]

    def x_send(m):
        for way in (1, -1):
            send(unit(fs_me, *pieces[m]), dev(dx=way), "x", way, m)


    def z_send(dx):
        for k in range(PARTS.get(dx, 1)):
            send(part(same(dx), u_me, k, dx), mirror, "z", dx, k)

    def share(f, *key):
        send(wt.at[f, rows_mine], sibling, "c", *key)

    def values_term(f, first=False):
        term = nn(inp[f], wt[f])
        vacc[...] = term if first else vacc[...] + term

    def input_grad(f):
        ig[f] = (nt(cot[...], wt[f]) + nn(back[...], dn[f])).astype(BF16)

    steps = {}

    def step(name):
        def keep_it(fn):
            steps[name] = fn
            return fn

        return keep_it

    @step("start")
    def _():
        loads["scales"].wait()
        scf[...] = scl[...].astype(F32)
        loads["codes"].wait()
        dequantize(c * 8 + u_me)
        loads["down"].wait()
        pl.semaphore_wait(barrier, len(peers))
        for d in (1, 3, 2):
            send(dpart(fs_me), dev(dx=d), "d1", d)
        send(dpart(fs_me), mirror, "d2")

    for m in range(5):
        steps[f"own{m}"] = functools.partial(x_send, m)
    steps["z0s"] = lambda: z_send(0)

    @step("own1")
    def _():
        dequantize(c * 8 + u_pair)
        x_send(1)

    @step("deq")
    def _():
        @pl.loop(1, 4)
        def _(d):
            for k in range(2):
                dequantize(c * 8 + 2 * lax.rem(y + d, 4) + k)

    @step("back")
    def _():
        loads["cot"].wait()
        loads["up"].wait()
        back[...] = (2.0 * nt(cot[...], upv[...])).astype(BF16)
        back_t[...] = (2.0 * nt(upv[...], cot[...])).astype(BF16)

    @step("rawdown")
    def _():
        for f in range(8):
            loads[("x", f)].wait()

        @pl.loop(0, 8)
        def _(f):
            raw[f] = nn(back_t[...], inp[f])

        send(raw.at[:, pl.ds(pl.multiple_of(32 - c * 32, 32), 32), :], sibling, "g1", dst=g1)

    @step("deq2")
    def _():
        loads["codes2"].wait()

        @pl.loop(0, 8)
        def _(k):
            dequantize((1 - c) * 8 + k)

    steps["mv_own"] = lambda: values_term(fs_me, first=True)
    steps["mi_own"] = lambda: input_grad(fs_me)

    @step("d1")
    def _():
        for d in (1, 3, 2):
            arrive(dpart(same(-d)), "d1", d)
        for d in (1, 2, 3):
            send(dpart(same(-d)), sibling, "d4", d)

    @step("d2")
    def _():
        arrive(dpart(other(0)), "d2")
        for d in (1, 3, 2):
            send(dpart(other(0)), dev(dx=d), "d3", d)
        send(dpart(other(0)), sibling, "d4", 0)

    @step("d3")
    def _():
        for d in (1, 3, 2):
            arrive(dpart(other(-d)), "d3", d)
            send(dpart(other(-d)), sibling, "d4", 3 + d)

    @step("low")
    def _():
        for d in (1, 2, 3):
            arrive(dpart(same(-d), cols_sib), "d4", d)
        arrive(dpart(other(0), cols_sib), "d4", 0)
        for d in (1, 2, 3):
            arrive(dpart(other(-d), cols_sib), "d4", 3 + d)
        low_t[...] = jnp.zeros_like(low_t)

        @pl.loop(0, 8)
        def _(f):
            low_t[...] += nt(dn[f], inp[f])

        up_term = 2.0 * nn(low_t[...].astype(BF16), cot[...])
        for f in range(8):
            raw_u[f] = up_term[:, f * 128 : f * 128 + 128]
        send(raw_u.at[:, pl.ds(pl.multiple_of(32 - c * 32, 32), 32), :], sibling, "h1", dst=g1_u)

    @step("low2")
    def _():
        low[...] = jnp.zeros_like(low)

        @pl.loop(0, 8)
        def _(f):
            low[...] += nt(inp[f], dn[f])

    keep, give = pl.ds(pl.multiple_of(r * 16, 16), 16), pl.ds(pl.multiple_of(16 - r * 16, 16), 16)
    keep_c = pl.ds(pl.multiple_of(c * 32 + r * 16, 16), 16)
    give_c = pl.ds(pl.multiple_of(c * 32 + 16 - r * 16, 16), 16)

    def reduce_steps(g, raw, g1, a2, b2, s2, a3, b3, s3, a4, b4):
        @step(g + "1")
        def _():
            arrive(g1, g + "1")

            @pl.loop(0, 8)
            def _(f):
                a2[f] = (raw[f, give_c, :] + g1[f, give, :]).astype(BF16)
                s2[f] = raw[f, keep_c, :] + g1[f, keep, :]

            send(a2, pair, g + "2", dst=b2)

        @step(g + "2")
        def _():
            arrive(b2, g + "2")
            for k in range(4):
                a3[k] = (s2[k * 2 + 1 - zh] + b2[k * 2 + 1 - zh].astype(F32)).astype(BF16)
            send(a3, mirror, g + "3", dst=b3)
            for k in range(4):
                s3[k] = s2[k * 2 + zh] + b2[k * 2 + zh].astype(F32)

        @step(g + "3")
        def _():
            arrive(b3, g + "3")
            for d in (1, 3, 2):
                k = lax.rem(x + d, 4)
                a4[d - 1] = (s3[k] + b3[k].astype(F32)).astype(BF16)
                send(a4.at[d - 1], dev(dx=d), g + "4", d, dst=b4.at[d - 1])

        def total():
            t = s3[x] + b3[x].astype(F32)
            for d in (1, 2, 3):
                arrive(b4.at[d - 1], g + "4", d)
                t += b4[d - 1].astype(F32)
            return t

        return total

    total_down = reduce_steps("g", raw, g1, a2, b2, s2, a3, b3, s3, a4, b4)
    total_up = reduce_steps("h", raw_u, g1_u, a2_u, b2_u, s2_u, a3_u, b3_u, s3_u, a4_u, b4_u)
    mine = y * 2 + lax.div(zl, 2)
    q = c * 2 + r
    others = [(d, flip) for d in (1, 3, 0, 2) for flip in range(2) if d or flip]

    @step("g4")
    def _():
        t5[mine, :, 0:1024] = total_down().astype(BF16)

    @step("h4")
    def _():
        t5[mine, :, 1024:EXT] = total_up().astype(BF16)
        for d, flip in others:
            send(t5.at[mine], dev(dy=d, zl_=3 - zl if flip else zl), "g5", d, flip)

    @step("g5")
    def _():
        for d, flip in others:
            at = lax.rem(y - d + 4, 4) * 2 + (1 - lax.div(zl, 2) if flip else lax.div(zl, 2))
            arrive(t5.at[at], "g5", d, flip)
        total = t5[0].astype(F32)
        for k in range(1, 8):
            total += t5[k].astype(F32)
        square = total * total
        square = square[0:8] + square[8:16]
        tile = square[:, 0:128]
        for k in range(1, 9):
            tile += square[:, k * 128 : k * 128 + 128]
        e6[fs_me, 0:16, :] = total[:, 1024:EXT]
        e6[fs_me, 16:24, :] = tile
        for d, flip in others:
            device = dev(dx=d, zl_=3 - zl, zh_=1 - zh) if flip else dev(dx=d)
            send(e6.at[fs_me], device, "g6", d, flip)
        f7[q, 0:16, :] = total[:, 0:1024]
        send(f7.at[q, 0:16], pair, "g7", 0)

    @step("g6")
    def _():
        for d, flip in others:
            at = other(-d) if flip else same(-d)
            arrive(e6.at[at], "g6", d, flip)
        tile = e6[0, 16:24, :]
        for f in range(8):
            f7[q, 16:32, f * 128 : f * 128 + 128] = e6[f, 0:16, :]
            if f:
                tile += e6[f, 16:24, :]
        f7[q, 32:40, 0:128] = tile
        f7[q, 32:40, 128:1024] = jnp.zeros((8, 896), F32)
        send(f7.at[q, 16:40], pair, "g7", 1)

    @step("g7")
    def _():
        arrive(f7.at[c * 2 + 1 - r, 0:16], "g7", 0)
        arrive(f7.at[c * 2 + 1 - r, 16:40], "g7", 1)
        send(f7.at[pl.ds(c * 2, 2)], sibling, "g8")

    @step("g8")
    def _():
        arrive(f7.at[pl.ds(2 - c * 2, 2)], "g8")
        tile = f7[0, 32:40, 0:128]
        for k in range(1, 4):
            tile += f7[k, 32:40, 0:128]
        squares = jnp.sum(jnp.sum(tile, axis=1, keepdims=True), axis=0, keepdims=True)
        factor = jnp.minimum(1.0, limit / jnp.sqrt(squares))
        for k in range(4):
            dgo[k * 16 : k * 16 + 16, :] = factor * f7[k, 0:16, :]
            ugo[k * 16 : k * 16 + 16, :] = factor * f7[k, 16:32, :]

    onward = {1: ((0, 0, 1), (2, 0, 2), (4, 0, 1)), -1: ((1, 0, 1), (3, 0, 2), (4, 1, 1))}

    def from_x(way, m):
        arrive(unit(same(-way), *pieces[m]), "x", way, m)
        for k, first, n in onward[way]:
            if k == m:
                send(unit(same(-way), pieces[m][0] + first, n), dev(dx=way), "xf", m, first)
        if m == 0:
            z_send(-way)

    def far_arrive(m, first, n):
        arrive(unit(same(2), pieces[m][0] + first, n), "xf", m, first)

    for m in range(5):
        steps[f"x+{m}"] = functools.partial(from_x, 1, m)
        steps[f"x-{m}"] = functools.partial(from_x, -1, m)

    @step("xf0")
    def _():
        far_arrive(0, 0, 1)
        z_send(2)

    @step("ss2")
    def _():
        for m, first, n in ((1, 0, 1), (2, 0, 2), (3, 0, 2), (4, 0, 1), (4, 1, 1)):
            far_arrive(m, first, n)
        share(same(2), "s", 2)

    fine = {dx: [] for dx in FINE}

    def other_steps(dx, by_pair, way, p):
        f, n_parts = other(dx), PARTS.get(dx, 1)
        q = f"{dx}" if n_parts == 1 else f"{dx}{'ab'[p]}"

        def piece(u):
            return part(f, u, p, dx)

        def take(u, *key):
            arrive(piece(u), *key)
            if dx in fine:
                send(piece(u), sibling, "f", dx, len(fine[dx]))
                fine[dx].append((u, p))

        @step(f"z{q}")
        def _():
            arrive(piece(u_me), "z", dx, p)
            if not by_pair:
                send(piece(u_me), pair, "p", dx, p)
            for w in (1, -1):
                send(piece(u_me), dev(dy=w), "y0", w, dx, p)
            if by_pair:
                send(piece(u_me), pair, "p", dx, p)
            if dx in fine:
                send(piece(u_me), sibling, "f", dx, len(fine[dx]))
                fine[dx].append((u_me, p))

        if by_pair:
            for w in (1, -1):

                @step(f"y0{w}_{q}")
                def _(w=w):
                    arrive(piece(chunk(-w) + r), "y0", w, dx, p)
                    if w == way:
                        send(piece(chunk(-w) + r), dev(dy=w), "yf", dx, p)
                    send(piece(chunk(-w) + r), pair, "pb", w, dx, p)
                    if dx in fine:
                        send(piece(chunk(-w) + r), sibling, "f", dx, len(fine[dx]))
                        fine[dx].append((chunk(-w) + r, p))

            @step(f"yf_{q}")
            def _():
                arrive(piece(chunk(2) + r), "yf", dx, p)
                send(piece(chunk(2) + r), pair, "pb", 0, dx, p)
                if dx in fine:
                    send(piece(chunk(2) + r), sibling, "f", dx, len(fine[dx]))
                    fine[dx].append((chunk(2) + r, p))

            def rest():
                take(u_pair, "p", dx, p)
                for w, d in ((1, -1), (-1, 1), (0, 2)):
                    take(chunk(d) + 1 - r, "pb", w, dx, p)

        else:

            @step(f"p{q}")
            def _():
                arrive(piece(u_pair), "p", dx, p)
                for w in (1, -1):
                    send(piece(u_pair), dev(dy=w), "y1", w, dx, p)
                if dx in fine:
                    send(piece(u_pair), sibling, "f", dx, len(fine[dx]))
                    fine[dx].append((u_pair, p))

            @step(f"y01_{q}")
            def _():
                arrive(piece(chunk(-1) + r), "y0", 1, dx, p)
                if dx in (0, 2):
                    send(piece(chunk(-1) + r), dev(dy=1), "yf0", dx, p)
                if dx in fine:
                    send(piece(chunk(-1) + r), sibling, "f", dx, len(fine[dx]))
                    fine[dx].append((chunk(-1) + r, p))

            @step(f"y1-1_{q}")
            def _():
                arrive(piece(chunk(1) + 1 - r), "y1", -1, dx, p)
                if dx in (0, 2):
                    send(piece(chunk(1) + 1 - r), dev(dy=-1), "yf1", dx, p)
                if dx in fine:
                    send(piece(chunk(1) + 1 - r), sibling, "f", dx, len(fine[dx]))
                    fine[dx].append((chunk(1) + 1 - r, p))

            def rest():
                take(chunk(1) + r, "y0", -1, dx, p)
                take(chunk(-1) + 1 - r, "y1", 1, dx, p)
                if dx == 2:
                    take(chunk(2) + r, "yf0", dx, p)
                    take(chunk(2) + 1 - r, "yf1", dx, p)

        return rest

    @step("xo")
    def _():
        for p in range(PARTS.get(0, 1)):
            arrive(part(other(0), chunk(2) + r, p, 0), "yf0", 0, p)
            arrive(part(other(0), chunk(2) + 1 - r, p, 0), "yf1", 0, p)
        for way in (1, -1):
            send(unit(other(0), chunk(2), 2), dev(dx=way), "xo", way)

    def last_pieces(dx, rests):
        for rest in rests:
            rest()
        if dx in (1, -1):
            arrive(unit(other(dx), chunk(2), 2), "xo", -dx)
            if dx in fine:
                send(unit(other(dx), chunk(2), 2), sibling, "f", dx, "xo")
        if dx == 0 and dx in fine:
            send(unit(other(0), chunk(2), 2), sibling, "f", dx, "xo")
        if dx not in fine:
            share(other(dx), "o", dx)

    for dx in (0, -1, 1, 2):
        way = 1 if dx in BY_PAIR and BY_PAIR.index(dx) % 2 == 0 else -1
        rests = [other_steps(dx, dx in BY_PAIR, way, p) for p in range(PARTS.get(dx, 1))]
        steps[f"so{dx}"] = functools.partial(last_pieces, dx, rests)

    def to_values(kind, f, dx):
        if kind == "o" and dx in fine:
            for k, (u, p) in enumerate(fine[dx]):
                arrive(part(f, u, p, dx, 512 - half), "f", dx, k)
            if dx != 2:
                arrive(unit(f, chunk(2), 2, 512 - half), "f", dx, "xo")
        else:
            arrive(wt.at[f, rows_sib], "c", kind, dx)
        values_term(f)

    for dx in (-1, 1, 2, 0):
        if dx:
            steps[f"mvs{dx}"] = functools.partial(to_values, "s", same(dx), dx)
            steps[f"mis{dx}"] = functools.partial(input_grad, same(dx))
        steps[f"mvo{dx}"] = functools.partial(to_values, "o", other(dx), dx)
        steps[f"mio{dx}"] = functools.partial(input_grad, other(dx))
    for dx in (-1, 1):
        steps[f"ss{dx}"] = functools.partial(share, same(dx), "s", dx)

    for name in ORDER:
        steps.pop(name)()
    assert not steps
    vout[...] = (vacc[...] + 2.0 * nn(low[...].astype(BF16), upv[...])).astype(BF16)
    for copy in sends:
        copy.wait_send()
    assert len(names) <= N_RECV and len(sends) <= N_SEND


def place(vout, ig, dgo, ugo, val_hbm, ig_hbm, dg_hbm, ug_hbm, sems):
    copies = [pltpu.make_async_copy(ig.at[f], ig_hbm.at[:, pl.ds(f * 1024, 1024)], sems.at[f]) for f in range(8)]
    for k, (src, dst) in enumerate(((vout, val_hbm), (dgo, dg_hbm), (ugo, ug_hbm))):
        copies.append(pltpu.make_async_copy(src, dst, sems.at[8 + k]))
    for copy in copies:
        copy.start()
    for copy in copies:
        copy.wait()


def local(*arguments):
    inputs, adapter_up = arguments[0], arguments[5]
    rank, values_width = adapter_up.shape
    limit = math.sqrt(rank * (inputs.shape[1] + values_width))
    scratch = [
        pltpu.VMEM((8, 256, 1024), BF16),
        pltpu.VMEM((256, 1024), BF16),
        pltpu.VMEM((1024, 1024), BF16),
        pltpu.VMEM((16, 1024), BF16),
        pltpu.VMEM((16, 1024), F32),
        pltpu.VMEM((64, 1024), BF16),
        pltpu.VMEM((8, 1024, 1024), BF16),
        pltpu.VMEM((8, 64, 1024), BF16),
        pltpu.VMEM((8, 64, 1024), F32),
        pltpu.VMEM((8, 32, 1024), F32),
        pltpu.VMEM((8, 16, 1024), BF16),
        pltpu.VMEM((8, 16, 1024), BF16),
        pltpu.VMEM((8, 16, 1024), F32),
        pltpu.VMEM((4, 16, 1024), BF16),
        pltpu.VMEM((4, 16, 1024), BF16),
        pltpu.VMEM((4, 16, 1024), F32),
        pltpu.VMEM((3, 16, 1024), BF16),
        pltpu.VMEM((3, 16, 1024), BF16),
        pltpu.VMEM((8, 64, 128), F32),
        pltpu.VMEM((8, 32, 128), F32),
        pltpu.VMEM((8, 16, 128), BF16),
        pltpu.VMEM((8, 16, 128), BF16),
        pltpu.VMEM((8, 16, 128), F32),
        pltpu.VMEM((4, 16, 128), BF16),
        pltpu.VMEM((4, 16, 128), BF16),
        pltpu.VMEM((4, 16, 128), F32),
        pltpu.VMEM((3, 16, 128), BF16),
        pltpu.VMEM((3, 16, 128), BF16),
        pltpu.VMEM((8, 16, EXT), BF16),
        pltpu.VMEM((8, 24, 128), F32),
        pltpu.VMEM((4, 40, 1024), F32),
        pltpu.VMEM((256, 1024), F32),
        pltpu.VMEM((256, 64), BF16),
        pltpu.VMEM((64, 256), BF16),
        pltpu.VMEM((256, 64), F32),
        pltpu.VMEM((64, 256), F32),
        pltpu.SemaphoreType.DMA((16,)),
        pltpu.SemaphoreType.DMA((N_SEND,)),
        pltpu.SemaphoreType.DMA((N_RECV,)),
    ]
    hbm = pl.BlockSpec(memory_space=pl.ANY)
    results = pl.pallas_call(
        functools.partial(kernel, limit),
        out_shape=(
            pltpu.VMEM((256, 1024), BF16),
            pltpu.VMEM((8, 256, 1024), BF16),
            pltpu.VMEM((64, 1024), F32),
            pltpu.VMEM((64, 1024), F32),
        ),
        in_specs=[hbm] * 6,
        out_specs=(pl.BlockSpec(memory_space=pltpu.VMEM),) * 4,
        scratch_shapes=scratch,
        cost_estimate=pl.CostEstimate(flops=9_600_000_000, bytes_accessed=12_000_000, transcendentals=0),
        compiler_params=pltpu.CompilerParams(
            collective_id=0, has_side_effects=True, vmem_limit_bytes=38 << 20
        ),
    )(*(pltpu.with_memory_space_constraint(a, pltpu.HBM) for a in arguments))
    return pl.pallas_call(
        place,
        out_shape=(
            jax.ShapeDtypeStruct((256, 1024), BF16),
            jax.ShapeDtypeStruct((256, 8192), BF16),
            jax.ShapeDtypeStruct((64, 1024), F32),
            jax.ShapeDtypeStruct((64, 1024), F32),
        ),
        in_specs=[pl.BlockSpec(memory_space=pltpu.VMEM)] * 4,
        out_specs=(hbm,) * 4,
        scratch_shapes=[pltpu.SemaphoreType.DMA((11,))],
        compiler_params=pltpu.CompilerParams(vmem_limit_bytes=1 << 20),
    )(*(pltpu.with_memory_space_constraint(a, pltpu.VMEM) for a in results))


def solution(mesh):
    return jax.shard_map(
        local,
        mesh=mesh,
        in_specs=(
            P(("rep", "fsdp"), None),
            P(("rep", "fsdp"), None),
            P("fsdp", None),
            P("fsdp", None),
            P(None, "fsdp"),
            P(),
        ),
        out_specs=(P(("rep", "fsdp"), None), P(("rep", "fsdp"), None), P(None, "fsdp"), P()),
        check_vma=False,
    )
```
